32 devices in a mesh: band: 16 (over z, y, core), mp: 2 (over x).
Axes of the slice: x: 2, y: 2, z: 4, core: 2. Of those that a mesh axis runs over, the one named last changes fastest.
Arguments:
- grid_latent: bfloat16 [16384, 1024], P(('band', 'mp')), may hold values from -6 to 6
- grid_gain: float32 [1024], replicated, may hold values from 0.1 to 1.9
- hidden_in: bfloat16 [4096, 1024], P('band'), may hold values from -6 to 6
- hid_gain: float32 [1024], replicated, may hold values from 0.1 to 1.9
- enc_wq: bfloat16 [1024, 1024], P(None, 'mp'), may hold values from -8 to 8
- enc_wk: bfloat16 [1024, 1024], P(None, 'mp'), may hold values from -0.1875 to 0.1875
- enc_wv: bfloat16 [1024, 1024], P(None, 'mp'), may hold values from -0.1875 to 0.1875
- enc_wo: bfloat16 [1024, 1024], P('mp'), may hold values from -0.1875 to 0.1875
- enc_edges: int32 [4096, 32], P('band'), may hold values from 0 to 16383, as said below
- enc_counts: int32 [4096], P('band'), may hold values from 1 to 32
- proc_gain: float32 [1024], replicated, may hold values from 0.1 to 1.9
- proc_wq: bfloat16 [1024, 1024], P(None, 'mp'), may hold values from -8 to 8
- proc_wk: bfloat16 [1024, 1024], P(None, 'mp'), may hold values from -0.25 to 0.25
- proc_wv: bfloat16 [1024, 1024], P(None, 'mp'), may hold values from -0.1875 to 0.1875
- proc_wo: bfloat16 [1024, 1024], P('mp'), may hold values from -0.1875 to 0.1875
Outputs:
- mixed: bfloat16 [4096, 1024], P('band')
The draws below stay inside these ranges and needn't reach their ends.
Inputs may be any that keep to these rules, and one draw needn't show every extreme that they name: `enc_edges`: node n lies in band b = n // 256; each of its edges references a grid point from b * 1024 - 128 to (b + 1) * 1024 + 127. Slots at or beyond the node's count hold valid grid points as well.
All inputs are finite; a program needn't handle non-finite values.
Results may differ from the reference program's by a relative error of at most 0.02.
Values may be sent and summed in bfloat16 or wider, within the bound.
No kernel may reach another device: no remote copies, remote signals or barrier semaphores. Data moves between devices by JAX's collectives and lax.ppermute only.
A program may use at most 128 MiB of HBM per device.

```python
import jax
import jax.numpy as jnp
from jax import lax

D = 1024
HEADS = 16
K_SLOTS = 32
WIN = 128
NODE_BAND = 256
GRID_BAND = 1024
GRID = 16384
RIM = 128
NODES = 4096
N_BAND = 16
N_MP = 2


def draw_enc_edges(key, part):
    nodes = jnp.arange(NODES, dtype=jnp.int32)
    band = nodes // NODE_BAND
    slot = jnp.arange(K_SLOTS, dtype=jnp.int32)
    rim_offset = jax.random.randint(jax.random.fold_in(key, 3), (NODES, K_SLOTS), 0, RIM, dtype=jnp.int32)
    band_offset = jax.random.randint(jax.random.fold_in(key, 4), (NODES, K_SLOTS), 0, GRID_BAND, dtype=jnp.int32)
    lower = band[:, None] * GRID_BAND - RIM + rim_offset
    upper = (band[:, None] + 1) * GRID_BAND + rim_offset
    inside = band[:, None] * GRID_BAND + band_offset
    kind = (slot % 4)[None, :]
    chosen = jnp.where(kind == 0, lower, jnp.where(kind == 2, upper, inside))
    return jnp.clip(chosen, 0, GRID - 1).astype(jnp.int32)


def draw_enc_counts(key, part):
    counts = jax.random.randint(jax.random.fold_in(key, 5), (NODES,), 1, K_SLOTS + 1, dtype=jnp.int32)
    spot = jax.random.randint(jax.random.fold_in(key, 6), (), 0, NODES, dtype=jnp.int32)
    return jnp.where(jnp.arange(NODES, dtype=jnp.int32) == spot, K_SLOTS, counts).astype(jnp.int32)


def draw_enc_wq(key, part):
    drawn = jax.random.normal(jax.random.fold_in(key, 29), (D, D), jnp.float32) * D ** (-0.5)
    return jnp.clip(drawn, -8.0, 8.0).astype(jnp.bfloat16)


def shared_keys(key):
    return jax.random.normal(jax.random.fold_in(key, 17), (D, D), jnp.float32) * D ** (-0.5)


def draw_proc_wk(key, part):
    return jnp.clip(shared_keys(key), -0.25, 0.25).astype(jnp.bfloat16)


def draw_proc_wq(key, part):
    drawn = jax.random.normal(jax.random.fold_in(key, 23), (D, D), jnp.float32) * D ** (-0.5)
    return jnp.clip(drawn, -8.0, 8.0).astype(jnp.bfloat16)


def level_of(key, shape, cuts, low, high):
    def one(position, parts):
        steps = jax.random.uniform(jax.random.fold_in(jax.random.fold_in(key, 6), position), (parts,), jnp.float32, low / len(cuts), high / len(cuts))
        return jnp.repeat(jnp.exp(steps), shape[position] // parts).reshape((-1,) + (1,) * (len(shape) - position - 1))

    level = one(*cuts[0])
    for cut in cuts[1:]:
        level = level * one(*cut)
    return level


def noise(key, extent, scale, reach, cuts=(), kind=jnp.bfloat16):
    values = jax.random.normal(key, extent, jnp.float32) * scale
    if len(cuts) > 0:
        values = level_of(key, extent, cuts, -0.22, 0.18) * values
    return jnp.clip(values, min=-reach, max=reach).astype(kind)


def setup_inputs(seed: int = 0) -> dict:
    key_of = jax.random.split(jax.random.key(seed), 16)
    grid_latent = noise(key_of[0], (GRID, D), 1.0, 6.0, ((0, 32),))
    grid_gain = jnp.clip(1.0 + 0.18 * jax.random.normal(key_of[1], (D,), jnp.float32), 0.1, 1.9)
    hidden_in = noise(key_of[2], (NODES, D), 1.0, 6.0, ((0, 16),))
    hid_gain = jnp.clip(1.0 + 0.18 * jax.random.normal(key_of[3], (D,), jnp.float32), 0.1, 1.9)
    enc_wq = draw_enc_wq(jax.random.fold_in(key_of[15], 71), 0)
    enc_wk = noise(key_of[5], (D, D), D ** -0.5, 0.1875, ((1, 2),))
    enc_wv = noise(key_of[6], (D, D), D ** -0.5, 0.1875, ((1, 2),))
    enc_wo = noise(key_of[7], (D, D), D ** -0.5, 0.1875, ((0, 2),))
    enc_edges = draw_enc_edges(jax.random.fold_in(key_of[15], 71), 0)
    enc_counts = draw_enc_counts(jax.random.fold_in(key_of[15], 71), 0)
    proc_gain = jnp.clip(1.0 + 0.18 * jax.random.normal(key_of[10], (D,), jnp.float32), 0.1, 1.9)
    proc_wq = draw_proc_wq(jax.random.fold_in(key_of[15], 71), 0)
    proc_wk = draw_proc_wk(jax.random.fold_in(key_of[15], 71), 0)
    proc_wv = noise(key_of[13], (D, D), D ** -0.5, 0.1875, ((1, 2),))
    proc_wo = noise(key_of[14], (D, D), D ** -0.5, 0.1875, ((0, 2),))
    return {"grid_latent": grid_latent, "grid_gain": grid_gain, "hidden_in": hidden_in, "hid_gain": hid_gain, "enc_wq": enc_wq, "enc_wk": enc_wk, "enc_wv": enc_wv, "enc_wo": enc_wo, "enc_edges": enc_edges, "enc_counts": enc_counts, "proc_gain": proc_gain, "proc_wq": proc_wq, "proc_wk": proc_wk, "proc_wv": proc_wv, "proc_wo": proc_wo}


EPSILON = 1e-05

def layer_norm(values, gain):
    values = values.astype(jnp.float32)
    center = values - lax.optimization_barrier(jnp.mean(values, axis=-1, keepdims=True))
    spread = lax.optimization_barrier(jnp.mean(center * center, axis=-1, keepdims=True))
    return center * lax.rsqrt(spread + EPSILON) * gain

def softmax_rows(scores):
    top = lax.optimization_barrier(jnp.max(scores, axis=-1, keepdims=True))
    expd = jnp.exp(scores - top)
    return (expd / lax.optimization_barrier(jnp.sum(expd, axis=-1, keepdims=True))).astype(jnp.bfloat16)

def edge_attention(query, keys, values, valid):
    scale = query.shape[-1] ** (-0.5)
    scores = jnp.einsum('nhe,nshe->nhs', query.astype(jnp.float32), keys.astype(jnp.float32)) * scale
    scores = jnp.where(valid[:, None, :], scores, -jnp.inf)
    weights = softmax_rows(scores)
    out = jnp.einsum('nhs,nshe->nhe', weights.astype(jnp.float32), values.astype(jnp.float32))
    return out.astype(jnp.bfloat16)

def window_attention(query, keys, values, valid):
    scale = query.shape[-1] ** (-0.5)
    scores = jnp.einsum('nhe,mhe->nhm', query.astype(jnp.float32), keys.astype(jnp.float32)) * scale
    scores = jnp.where(valid[:, None, :], scores, -jnp.inf)
    weights = softmax_rows(scores)
    out = jnp.einsum('nhm,mhe->nhe', weights.astype(jnp.float32), values.astype(jnp.float32))
    return out.astype(jnp.bfloat16)

def head_sum(heads, w_out, groups):
    count = heads.shape[0]
    width = heads.shape[1] // groups
    pieces = heads.reshape(count, groups, width).astype(jnp.float32)
    blocks = w_out.reshape(groups, width, -1).astype(jnp.float32)
    partial_value = jnp.einsum('npc,pcd->npd', pieces, blocks).astype(jnp.bfloat16)
    return lax.optimization_barrier(jnp.sum(partial_value.astype(jnp.float32), axis=1))

def project(rows, weight):
    return jnp.dot(rows, weight, preferred_element_type=jnp.float32).astype(jnp.bfloat16)

def reference(grid_latent, grid_gain, hidden_in, hid_gain, enc_wq, enc_wk, enc_wv, enc_wo, enc_edges, enc_counts, proc_gain, proc_wq, proc_wk, proc_wv, proc_wo):
    head_dim = D // HEADS
    grid_norm = layer_norm(grid_latent, grid_gain).astype(jnp.bfloat16)
    enc_keys = project(grid_norm, enc_wk)
    enc_values = project(grid_norm, enc_wv)
    node_norm = layer_norm(hidden_in, hid_gain).astype(jnp.bfloat16)
    enc_query = project(node_norm, enc_wq)

    def encode_band(band):
        start = (band * NODE_BAND).astype(jnp.int32)
        rows = lax.dynamic_slice_in_dim(enc_query, start, NODE_BAND, 0).reshape(NODE_BAND, HEADS, head_dim)
        edges = lax.dynamic_slice_in_dim(enc_edges, start, NODE_BAND, 0).reshape(-1)
        counts = lax.dynamic_slice_in_dim(enc_counts, start, NODE_BAND, 0)
        near_keys = jnp.take(enc_keys, edges, axis=0).reshape(NODE_BAND, K_SLOTS, HEADS, head_dim)
        near_values = jnp.take(enc_values, edges, axis=0).reshape(NODE_BAND, K_SLOTS, HEADS, head_dim)
        valid = jnp.arange(K_SLOTS, dtype=jnp.int32)[None, :] < counts[:, None]
        heads = edge_attention(rows, near_keys, near_values, valid).reshape(NODE_BAND, D)
        base = lax.dynamic_slice_in_dim(hidden_in, start, NODE_BAND, 0).astype(jnp.float32)
        return base + head_sum(heads, enc_wo, N_MP)
    latent = lax.map(encode_band, jnp.arange(N_BAND, dtype=jnp.int32)).reshape(NODES, D)
    proc_norm = layer_norm(latent, proc_gain).astype(jnp.bfloat16)
    proc_query = project(proc_norm, proc_wq)
    proc_keys = project(proc_norm, proc_wk)
    proc_values = project(proc_norm, proc_wv)
    margin = jnp.zeros((WIN, D), jnp.bfloat16)
    keys_wide = jnp.concatenate([margin, proc_keys, margin], axis=0)
    values_wide = jnp.concatenate([margin, proc_values, margin], axis=0)
    span = NODE_BAND + 2 * WIN

    def window_band(band):
        start = (band * NODE_BAND).astype(jnp.int32)
        rows = lax.dynamic_slice_in_dim(proc_query, start, NODE_BAND, 0).reshape(NODE_BAND, HEADS, head_dim)
        keys = lax.dynamic_slice_in_dim(keys_wide, start, span, 0).reshape(span, HEADS, head_dim)
        values = lax.dynamic_slice_in_dim(values_wide, start, span, 0).reshape(span, HEADS, head_dim)
        own = start + jnp.arange(NODE_BAND, dtype=jnp.int32)
        other = start - WIN + jnp.arange(span, dtype=jnp.int32)
        valid = (jnp.abs(own[:, None] - other[None, :]) <= WIN) & (other >= 0)[None, :] & (other < NODES)[None, :]
        heads = window_attention(rows, keys, values, valid).reshape(NODE_BAND, D)
        base = lax.dynamic_slice_in_dim(latent, start, NODE_BAND, 0)
        return (base + head_sum(heads, proc_wo, N_MP)).astype(jnp.bfloat16)
    return lax.map(window_band, jnp.arange(N_BAND, dtype=jnp.int32)).reshape(NODES, D)
```

```python
import functools

import jax
import jax.numpy as jnp
from jax import lax
from jax.experimental import pallas as pl
from jax.experimental.pallas import tpu as pltpu
from jax.sharding import PartitionSpec as P

D = 1024
HEADS = 16
WIN = 128
HEAD_DIM = D // HEADS
LANES = 128

EPSILON = 1e-05
NEG = -1e30
VMEM_LIMIT = 48 * 1024 * 1024

f32 = jnp.float32
bf16 = jnp.bfloat16


def whole(shape):
    return pl.BlockSpec(shape, lambda: (0,) * len(shape))


def call(kernel, outs, args, scratch=(), flops=0):
    moved = sum(a.size * a.dtype.itemsize for a in args)
    moved += sum(o.size * o.dtype.itemsize for o in outs)
    return pl.pallas_call(
        kernel,
        out_shape=outs,
        in_specs=[whole(a.shape) for a in args],
        out_specs=[whole(o.shape) for o in outs],
        scratch_shapes=list(scratch),
        compiler_params=pltpu.CompilerParams(vmem_limit_bytes=VMEM_LIMIT),
        cost_estimate=pl.CostEstimate(flops=flops, bytes_accessed=moved, transcendentals=0),
    )(*args)


def shape_of(*shape, dtype):
    return jax.ShapeDtypeStruct(shape, dtype)


def layer_norm(values, gain):
    values = values.astype(f32)
    center = values - jnp.mean(values, axis=-1, keepdims=True)
    spread = jnp.mean(center * center, axis=-1, keepdims=True)
    return center * lax.rsqrt(spread + EPSILON) * gain


def dot(a, b):
    return jnp.dot(a, b, preferred_element_type=f32)


def dot_nt(a, b):
    return lax.dot_general(a, b, (((1,), (1,)), ((), ())), preferred_element_type=f32)


def norm_rows(src, gain, dst, base, block=64):
    rows = src.shape[0]
    block = min(block, rows)

    def step(i, carry):
        at = pl.ds(pl.multiple_of(i * block, block), block)
        to = pl.ds(pl.multiple_of(base + i * block, block), block)
        dst[to, :] = layer_norm(src[at, :], gain[...]).astype(bf16)
        return carry

    lax.fori_loop(0, rows // block, step, 0)


def even_lanes(rows):
    return lax.broadcasted_iota(jnp.int32, (rows, LANES), 1) < HEAD_DIM


def two_heads(pair):
    even = even_lanes(pair.shape[0])
    zero = jnp.zeros_like(pair)
    return jnp.concatenate([jnp.where(even, pair, zero), jnp.where(even, zero, pair)], axis=0)


def fold_heads(stacked):
    rows = stacked.shape[0] // 2
    return jnp.where(even_lanes(rows), stacked[:rows], stacked[rows:])


def attend(query, parts):
    both = two_heads(query)
    scores = []
    top = None
    for keys, _, bias in parts:
        part = dot_nt(both, keys)
        if bias is not None:
            part = part + jnp.concatenate([bias, bias], axis=0)
        scores.append(part)
        peak = jnp.max(part, axis=1, keepdims=True)
        top = peak if top is None else jnp.maximum(top, peak)
    out = None
    for (_, values, _), part in zip(parts, scores):
        weights = jnp.exp(part - top).astype(bf16)
        wide = jnp.concatenate([values, jnp.ones_like(values)], axis=1)
        add = dot(weights, wide)
        out = add if out is None else out + add
    top = jnp.broadcast_to(top, (top.shape[0], LANES))
    return fold_heads(out[:, :LANES]), fold_heads(out[:, LANES:]), fold_heads(top)


def merge(one, two):
    out1, sum1, top1 = one
    out2, sum2, top2 = two
    top = jnp.maximum(top1, top2)
    keep1 = jnp.exp(top1 - top)
    keep2 = jnp.exp(top2 - top)
    return out1 * keep1 + out2 * keep2, sum1 * keep1 + sum2 * keep2, top


def prep_kernel(sizes, place, hidden, gain, wq, *refs):
    logs, (query, norm) = refs[: len(sizes)], refs[len(sizes) :]
    groups, width = place.shape
    nodes = 8
    slots = width // nodes
    blocks = sum(sizes) // LANES
    row_hi = lax.broadcasted_iota(jnp.int32, (blocks * nodes, width), 0)
    row_lo = lax.broadcasted_iota(jnp.int32, (LANES, width), 0)
    node = lax.broadcasted_iota(jnp.int32, (1, width), 1) // slots

    def step(g, carry):
        at = place[pl.ds(g, 1), :]
        high = jnp.where(at < 0, -1, (at // LANES) * nodes + node)
        left = (row_hi == high).astype(f32).astype(bf16)
        right = (row_lo == at % LANES).astype(f32).astype(bf16)
        count = dot_nt(left, right)
        count = jnp.where(count > 0, jnp.log(jnp.maximum(count, 1.0)), NEG)
        rows = pl.ds(pl.multiple_of(g * nodes, nodes), nodes)
        block = 0
        for log, size in zip(logs, sizes):
            for c in range(size // LANES):
                log[rows, c * LANES : (c + 1) * LANES] = count[block * nodes : (block + 1) * nodes]
                block += 1
        return carry

    lax.fori_loop(0, groups, step, 0)
    norm_rows(hidden, gain, norm, 0)
    scaled = dot(norm[...], wq[...]).astype(bf16) * (HEAD_DIM**-0.5)
    query[...] = scaled.astype(bf16)


def grid_kernel(count, first, last, *refs):
    refs = list(refs)
    rows = [refs.pop(0) for _ in range(count)]
    logs = [refs.pop(0) for _ in range(count)]
    gain, wk, wv, query = [refs.pop(0) for _ in range(4)]
    before = None if first else [refs.pop(0) for _ in range(3)]
    if last:
        wo, share = refs.pop(0), refs.pop(0)
    else:
        after = [refs.pop(0) for _ in range(3)]
    norm, keys, values = refs[:3]
    heads = refs[3] if last else None
    base = 0
    for r in rows:
        norm_rows(r, gain, norm, base)
        base += r.shape[0]
    keys[...] = dot(norm[...], wk[...]).astype(bf16)
    values[...] = dot(norm[...], wv[...]).astype(bf16)
    for p in range(query.shape[1] // LANES):
        cols = slice(p * LANES, (p + 1) * LANES)
        parts = []
        base = 0
        for r, log in zip(rows, logs):
            at = slice(base, base + r.shape[0])
            parts.append((keys[at, cols], values[at, cols], log[...]))
            base += r.shape[0]
        state = attend(query[:, cols], parts)
        if before is not None:
            state = merge([b[:, cols] for b in before], state)
        if last:
            heads[:, cols] = (state[0] / state[1]).astype(bf16)
        else:
            for ref, value in zip(after, state):
                ref[:, cols] = value
    if last:
        share[...] = dot(heads[...], wo[...]).astype(bf16)


def grid_attention(rows, logs, gain, wk, wv, query, before=None, wo=None):
    total = sum(r.shape[0] for r in rows)
    nodes, columns = query.shape
    last = wo is not None
    args = [*rows, *logs, gain, wk, wv, query, *(before or []), *([wo] if last else [])]
    if last:
        outs = [shape_of(nodes, wo.shape[1], dtype=bf16)]
    else:
        outs = [shape_of(nodes, columns, dtype=f32)] * 3
    scratch = [
        pltpu.VMEM((total, wk.shape[0]), bf16),
        pltpu.VMEM((total, columns), bf16),
        pltpu.VMEM((total, columns), bf16),
    ]
    if last:
        scratch.append(pltpu.VMEM((nodes, columns), bf16))
    kernel = functools.partial(grid_kernel, len(rows), before is None, last)
    flops = 4 * total * wk.size + 16 * nodes * total * columns
    return call(kernel, outs, args, scratch, flops)


def node_kernel(hidden, own, other, gain, wq, wk, wv, query, low, high, norm):
    latent = hidden[...].astype(f32) + (own[...].astype(f32) + other[...].astype(f32))
    norm[...] = layer_norm(latent, gain[...]).astype(bf16)
    rows, columns = query.shape
    scaled = dot(norm[...], wq[...]).astype(bf16) * (HEAD_DIM**-0.5)
    query[...] = scaled.astype(bf16)
    for weight, at in ((wk, 0), (wv, columns)):
        value = dot(norm[...], weight[...]).astype(bf16)
        low[:, at : at + columns] = value[: rows // 2]
        high[:, at : at + columns] = value[rows // 2 :]


def window_bias(queries, keys, shift):
    i = lax.broadcasted_iota(jnp.int32, (queries, keys), 0)
    j = lax.broadcasted_iota(jnp.int32, (queries, keys), 1) + shift
    return jnp.where(jnp.abs(i - j) <= WIN, 0.0, NEG).astype(f32)


def own_kernel(query, low, high, out, total, top):
    rows, columns = query.shape
    half = low.shape[0]
    bias_low = window_bias(rows, half, 0)
    bias_high = window_bias(rows, half, half)
    for p in range(columns // LANES):
        cols = slice(p * LANES, (p + 1) * LANES)
        vals = slice(columns + p * LANES, columns + (p + 1) * LANES)
        parts = [
            (low[:, cols], low[:, vals], bias_low),
            (high[:, cols], high[:, vals], bias_high),
        ]
        for ref, value in zip((out, total, top), attend(query[:, cols], parts)):
            ref[:, cols] = value


def halo_kernel(ends, query, before, after, out, total, top, wo, share, heads):
    rows, columns = query.shape
    bias_before = window_bias(WIN, WIN, -WIN) + jnp.where(ends[0] == 0, NEG, 0.0)
    bias_after = window_bias(WIN, WIN, WIN) + jnp.where(ends[1] == 0, NEG, 0.0)
    for p in range(columns // LANES):
        cols = slice(p * LANES, (p + 1) * LANES)
        vals = slice(columns + p * LANES, columns + (p + 1) * LANES)
        state = [ref[:, cols] for ref in (out, total, top)]
        side = attend(query[:WIN, cols], [(before[:, cols], before[:, vals], bias_before)])
        first = merge([s[:WIN] for s in state], side)
        state = [jnp.concatenate([f, s[WIN:]], axis=0) for f, s in zip(first, state)]
        side = attend(query[rows - WIN :, cols], [(after[:, cols], after[:, vals], bias_after)])
        final = merge([s[rows - WIN :] for s in state], side)
        state = [jnp.concatenate([s[: rows - WIN], f], axis=0) for f, s in zip(final, state)]
        heads[:, cols] = (state[0] / state[1]).astype(bf16)
    share[...] = dot(heads[...], wo[...]).astype(bf16)


def mixed_kernel(hidden, own, other, own_share, other_share, mixed):
    latent = hidden[...].astype(f32) + (own[...].astype(f32) + other[...].astype(f32))
    mixed[...] = (latent + (own_share[...].astype(f32) + other_share[...].astype(f32))).astype(bf16)


def shards(
    grid_latent,
    grid_gain,
    hidden_in,
    hid_gain,
    enc_wq,
    enc_wk,
    enc_wv,
    enc_wo,
    enc_edges,
    enc_counts,
    proc_gain,
    proc_wq,
    proc_wk,
    proc_wv,
    proc_wo,
):
    band, bands = lax.axis_index("band"), lax.axis_size("band")
    me, peers = lax.axis_index("mp"), lax.axis_size("mp")
    rows = grid_latent.shape[0]
    grid_band = rows * peers
    rim = grid_band // 8
    nodes, slots = enc_edges.shape
    columns = enc_wk.shape[1]
    up = [(i, i + 1) for i in range(bands - 1)]
    down = [(i + 1, i) for i in range(bands - 1)]
    grid_gain, hid_gain, proc_gain = [g.reshape(1, -1) for g in (grid_gain, hid_gain, proc_gain)]

    def shifted(value, by):
        return lax.ppermute(value, "mp", [((i + by) % peers, i) for i in range(peers)])

    at = enc_edges - band * grid_band
    owner, inner = at // rows, at % rows
    ahead = (owner - me) % peers
    if peers == 2:
        cut = min(rows - rim, max(LANES, (rows - rim) // 3 * 2 // LANES * LANES))
        mine = jnp.where(me == 0, 0, rows - rim)
        edge = shifted(lax.dynamic_slice_in_dim(grid_latent, mine, rim, 0), 1)
        rest = jnp.where(me == 0, rim, 0)
        middle = shifted(lax.dynamic_slice_in_dim(grid_latent, rest, cut, 0), 1)
        final = shifted(lax.dynamic_slice_in_dim(grid_latent, rest + cut, rows - rim - cut, 0), 1)
        after_band = jnp.where(me == 0, grid_latent[:rim], edge)
        before_band = jnp.where(me == 0, edge, grid_latent[rows - rim :])
        theirs = jnp.where(owner == 0, 0, rows - rim)
        inner = jnp.where(ahead == 0, inner, (inner - theirs) % rows)
        pieces = [grid_latent, edge, middle, final]
    else:
        pieces = [grid_latent] + [shifted(grid_latent, d) for d in range(1, peers)]
        stack = jnp.stack(pieces)
        after_band = lax.dynamic_index_in_dim(stack, (-me) % peers, 0, False)[:rim]
        before_band = lax.dynamic_index_in_dim(stack, (peers - 1 - me) % peers, 0, False)[rows - rim :]
    lower = lax.ppermute(before_band, "band", up)
    upper = lax.ppermute(after_band, "band", down)
    pieces += [lower, upper]
    sizes = [p.shape[0] for p in pieces]
    place = jnp.where(at < 0, grid_band + rim + at, ahead * rows + inner)
    place = jnp.where(at >= grid_band, rim + at, place)
    live = jnp.arange(slots, dtype=jnp.int32)[None, :] < enc_counts[:, None]
    place = jnp.where(live, place, -1).reshape(nodes // 8, 8 * slots)

    *logs, query = call(
        functools.partial(prep_kernel, sizes),
        [shape_of(nodes, s, dtype=f32) for s in sizes] + [shape_of(nodes, columns, dtype=bf16)],
        [place, hidden_in, hid_gain, enc_wq],
        [pltpu.VMEM((nodes, hidden_in.shape[1]), bf16)],
        2 * nodes * enc_wq.size,
    )
    encode = functools.partial(grid_attention, gain=grid_gain, wk=enc_wk, wv=enc_wv, query=query)
    if peers == 2:
        order = [[0], [1, 4, 5, 2], [3]]
    else:
        order = [[i] for i in range(len(pieces))]
    state = None
    for i, group in enumerate(order):
        wo = enc_wo if i == len(order) - 1 else None
        state = encode([pieces[k] for k in group], [logs[k] for k in group], before=state, wo=wo)
    (own,) = state

    def exchange(share):
        if peers == 2:
            return shifted(share, 1)
        total = lax.psum(share.astype(f32), "mp")
        return total - share.astype(f32)

    other = exchange(own)
    query, low, high = call(
        node_kernel,
        [
            shape_of(nodes, columns, dtype=bf16),
            shape_of(nodes // 2, 2 * columns, dtype=bf16),
            shape_of(nodes // 2, 2 * columns, dtype=bf16),
        ],
        [hidden_in, own, other, proc_gain, proc_wq, proc_wk, proc_wv],
        [pltpu.VMEM(hidden_in.shape, bf16)],
        6 * nodes * proc_wq.size,
    )
    before = lax.ppermute(high, "band", up)
    after = lax.ppermute(low, "band", down)
    state = call(
        own_kernel,
        [shape_of(nodes, columns, dtype=f32)] * 3,
        [query, low, high],
        (),
        16 * nodes * nodes * columns,
    )
    ends = jnp.stack([band > 0, band < bands - 1]).astype(jnp.int32)
    smem = pl.BlockSpec(memory_space=pltpu.SMEM)
    args = [ends, query, before, after, *state, proc_wo]
    (own_share,) = pl.pallas_call(
        halo_kernel,
        out_shape=[shape_of(nodes, proc_wo.shape[1], dtype=bf16)],
        in_specs=[smem] + [whole(a.shape) for a in args[1:]],
        out_specs=[whole((nodes, proc_wo.shape[1]))],
        scratch_shapes=[pltpu.VMEM((nodes, columns), bf16)],
        compiler_params=pltpu.CompilerParams(vmem_limit_bytes=VMEM_LIMIT),
    )(*args)
    other_share = exchange(own_share)
    (mixed,) = call(
        mixed_kernel,
        [shape_of(*hidden_in.shape, dtype=bf16)],
        [hidden_in, own, other, own_share, other_share],
    )
    return mixed


def solution(mesh):
    return jax.shard_map(
        shards,
        mesh=mesh,
        in_specs=(
            P(("band", "mp"), None),
            P(),
            P("band", None),
            P(),
            P(None, "mp"),
            P(None, "mp"),
            P(None, "mp"),
            P("mp", None),
            P("band", None),
            P("band"),
            P(),
            P(None, "mp"),
            P(None, "mp"),
            P(None, "mp"),
            P("mp", None),
        ),
        out_specs=P("band", None),
        check_vma=False,
    )
```

```python
import functools

import jax
import jax.numpy as jnp
from jax import lax
from jax.experimental import pallas as pl
from jax.experimental.pallas import tpu as pltpu
from jax.sharding import PartitionSpec as P

D = 1024
HEADS = 16
WIN = 128
HEAD_DIM = D // HEADS
LANES = 128

EPSILON = 1e-05
NEG = -1e30
VMEM_LIMIT = 48 * 1024 * 1024

f32 = jnp.float32
bf16 = jnp.bfloat16


def whole(shape):
    return pl.BlockSpec(shape, lambda: (0,) * len(shape))


def call(kernel, outs, args, scratch=(), flops=0):
    moved = sum(a.size * a.dtype.itemsize for a in args)
    moved += sum(o.size * o.dtype.itemsize for o in outs)
    return pl.pallas_call(
        kernel,
        out_shape=outs,
        in_specs=[whole(a.shape) for a in args],
        out_specs=[whole(o.shape) for o in outs],
        scratch_shapes=list(scratch),
        compiler_params=pltpu.CompilerParams(vmem_limit_bytes=VMEM_LIMIT),
        cost_estimate=pl.CostEstimate(flops=flops, bytes_accessed=moved, transcendentals=0),
    )(*args)


def shape_of(*shape, dtype):
    return jax.ShapeDtypeStruct(shape, dtype)


def layer_norm(values, gain):
    values = values.astype(f32)
    center = values - jnp.mean(values, axis=-1, keepdims=True)
    spread = jnp.mean(center * center, axis=-1, keepdims=True)
    return center * lax.rsqrt(spread + EPSILON) * gain


def dot(a, b):
    return jnp.dot(a, b, preferred_element_type=f32)


def dot_nt(a, b):
    return lax.dot_general(a, b, (((1,), (1,)), ((), ())), preferred_element_type=f32)


def norm_rows(src, gain, dst, base, block=64):
    rows = src.shape[0]
    block = min(block, rows)

    def step(i, carry):
        at = pl.ds(pl.multiple_of(i * block, block), block)
        to = pl.ds(pl.multiple_of(base + i * block, block), block)
        dst[to, :] = layer_norm(src[at, :], gain[...]).astype(bf16)
        return carry

    lax.fori_loop(0, rows // block, step, 0, unroll=2 if rows // block % 2 == 0 else 1)


def even_lanes(rows):
    return lax.broadcasted_iota(jnp.int32, (rows, LANES), 1) < HEAD_DIM


def two_heads(pair):
    even = even_lanes(pair.shape[0])
    zero = jnp.zeros_like(pair)
    return jnp.concatenate([jnp.where(even, pair, zero), jnp.where(even, zero, pair)], axis=0)


def fold_heads(stacked):
    rows = stacked.shape[0] // 2
    return jnp.where(even_lanes(rows), stacked[:rows], stacked[rows:])


def attend(query, parts):
    both = two_heads(query)
    scores = []
    top = None
    for keys, _, bias in parts:
        part = dot_nt(both, keys)
        if bias is not None:
            part = part + jnp.concatenate([bias, bias], axis=0)
        scores.append(part)
        peak = jnp.max(part, axis=1, keepdims=True)
        top = peak if top is None else jnp.maximum(top, peak)
    out = None
    for (_, values, _), part in zip(parts, scores):
        weights = jnp.exp(part - top).astype(bf16)
        wide = jnp.concatenate([values, jnp.ones_like(values)], axis=1)
        add = dot(weights, wide)
        out = add if out is None else out + add
    top = jnp.broadcast_to(top, (top.shape[0], LANES))
    return fold_heads(out[:, :LANES]), fold_heads(out[:, LANES:]), fold_heads(top)


def merge(one, two):
    out1, sum1, top1 = one
    out2, sum2, top2 = two
    top = jnp.maximum(top1, top2)
    keep1 = jnp.exp(top1 - top)
    keep2 = jnp.exp(top2 - top)
    return out1 * keep1 + out2 * keep2, sum1 * keep1 + sum2 * keep2, top


def pick_kernel(cuts, whole_refs, outs, sems):
    copies = [
        pltpu.make_async_copy(
            whole_refs[k].at[pl.ds(pl.multiple_of(start(), 16), out.shape[0])], out, sems.at[i]
        )
        for i, ((k, start), out) in enumerate(zip(cuts, outs))
    ]
    for copy in copies:
        copy.start()
    for copy in copies:
        copy.wait()


def pick(arrays, cuts):
    def kernel(*refs):
        n = len(arrays)
        pick_kernel([(k, start) for k, start, _ in cuts], refs[:n], refs[n:-1], refs[-1])

    outs = [shape_of(count, arrays[k].shape[1], dtype=arrays[k].dtype) for k, _, count in cuts]
    moved = 2 * sum(o.size * o.dtype.itemsize for o in outs)
    return pl.pallas_call(
        kernel,
        out_shape=outs,
        in_specs=[pl.BlockSpec(memory_space=pltpu.HBM)] * len(arrays),
        out_specs=[whole(o.shape) for o in outs],
        scratch_shapes=[pltpu.SemaphoreType.DMA((len(cuts),))],
        compiler_params=pltpu.CompilerParams(vmem_limit_bytes=VMEM_LIMIT),
        cost_estimate=pl.CostEstimate(flops=0, bytes_accessed=moved, transcendentals=0),
    )(*arrays)


def place_of(edges, rows, rim, peers):
    band, me = lax.axis_index("band"), lax.axis_index("mp")
    grid_band = rows * peers
    at = edges - band * grid_band
    owner, inner = at // rows, at % rows
    ahead = lax.rem(owner - me + peers, peers)
    if peers == 2:
        turn = jnp.where(owner == 0, 0, rim)
        inner = jnp.where(ahead == 0, inner, (inner + turn) % rows)
        lower = grid_band + (1 - me) * rim
        upper = grid_band + me * rim
    else:
        lower = grid_band
        upper = grid_band + rim
    place = jnp.where(at < 0, lower + rim + at, ahead * rows + inner)
    return jnp.where(at >= grid_band, upper + at - grid_band, place)


def prep_kernel(sizes, rows, rim, peers, edges, counts, hidden, gain, wq, *refs):
    logs, (query, norm, turned, line) = refs[: len(sizes)], refs[len(sizes) :]
    slots, nodes = edges.shape
    share = 8
    width = share * slots
    blocks = sum(sizes) // LANES
    place = place_of(edges[...], rows, rim, peers)
    live = lax.broadcasted_iota(jnp.int32, (slots, nodes), 0) < counts[...]
    node = lax.broadcasted_iota(jnp.int32, (slots, nodes), 1) % share
    high = jnp.where(live, (place // LANES) * share + node, -1)
    turned[...] = (high * LANES + place % LANES).T
    line[...] = jnp.concatenate(
        [turned[pl.ds(i, nodes // share, stride=share), :] for i in range(share)], axis=1
    )
    row_hi = lax.broadcasted_iota(jnp.int32, (blocks * share, width), 0)
    row_lo = lax.broadcasted_iota(jnp.int32, (LANES, width), 0)

    def step(g, carry):
        code = line[pl.ds(g, 1), :]
        left = (row_hi == (code >> 7)).astype(f32).astype(bf16)
        right = (row_lo == (code & (LANES - 1))).astype(f32).astype(bf16)
        count = dot_nt(left, right)
        count = jnp.where(count > 0, jnp.log(jnp.maximum(count, 1.0)), NEG)
        to = pl.ds(pl.multiple_of(g * share, share), share)
        block = 0
        for log, size in zip(logs, sizes):
            for c in range(size // LANES):
                log[to, c * LANES : (c + 1) * LANES] = count[block * share : (block + 1) * share]
                block += 1
        return carry

    lax.fori_loop(0, nodes // share, step, 0, unroll=4)
    norm_rows(hidden, gain, norm, 0)
    scaled = dot(norm[...], wq[...]).astype(bf16) * (HEAD_DIM**-0.5)
    query[...] = scaled.astype(bf16)


def encode_heads(query, log, keys, values, before, at, heads):
    for p in range(query.shape[1] // LANES):
        cols = slice(p * LANES, (p + 1) * LANES)
        state = attend(query[at, cols], [(keys[:, cols], values[:, cols], log[at, :])])
        if before is not None:
            state = merge([b[at, cols] for b in before], state)
        heads[:, cols] = (state[0] / state[1]).astype(bf16)


def grid_kernel(count, first, last, *refs):
    refs = list(refs)
    rows = [refs.pop(0) for _ in range(count)]
    log, gain, wk, wv, query = [refs.pop(0) for _ in range(5)]
    before = None if first else [refs.pop(0) for _ in range(3)]
    if last:
        wo, share, keys, values, norm, heads = refs
    else:
        *after, norm, keys, values = refs
    base = 0
    for r in rows:
        norm_rows(r, gain, norm, base)
        base += r.shape[0]
    keys[...] = dot(norm[...], wk[...]).astype(bf16)
    values[...] = dot(norm[...], wv[...]).astype(bf16)
    if last:
        encode_heads(query, log, keys, values, before, slice(0, heads.shape[0]), heads)
        share[...] = dot(heads[...], wo[...]).astype(bf16)
        return
    for p in range(query.shape[1] // LANES):
        cols = slice(p * LANES, (p + 1) * LANES)
        state = attend(query[:, cols], [(keys[:, cols], values[:, cols], log[...])])
        if before is not None:
            state = merge([b[:, cols] for b in before], state)
        for ref, value in zip(after, state):
            ref[:, cols] = value


def grid_attention(rows, log, gain, wk, wv, query, before=None, wo=None):
    total = sum(r.shape[0] for r in rows)
    nodes, columns = query.shape
    args = [*rows, log, gain, wk, wv, query, *(before or []), *([] if wo is None else [wo])]
    pair = (total, columns)
    norm = pltpu.VMEM((total, wk.shape[0]), bf16)
    if wo is None:
        outs = [shape_of(nodes, columns, dtype=f32)] * 3
        scratch = [norm, pltpu.VMEM(pair, bf16), pltpu.VMEM(pair, bf16)]
    else:
        outs = [shape_of(nodes // 2, wo.shape[1], dtype=bf16)] + [shape_of(*pair, dtype=bf16)] * 2
        scratch = [norm, pltpu.VMEM((nodes // 2, columns), bf16)]
    kernel = functools.partial(grid_kernel, len(rows), before is None, wo is not None)
    flops = 4 * total * wk.size + 16 * nodes * total * columns
    return call(kernel, outs, args, scratch, flops)


def rest_kernel(log, query, keys, values, out, total, top, wo, share, heads):
    half = heads.shape[0]
    encode_heads(query, log, keys, values, (out, total, top), slice(half, 2 * half), heads)
    share[...] = dot(heads[...], wo[...]).astype(bf16)


def latent_of(at, hidden, own, other):
    total = own[...].astype(f32) + other[...].astype(f32)
    return hidden[at : at + own.shape[0], :].astype(f32) + total


def node_kernel(at, hidden, own, other, gain, wq, wk, wv, query, pair, norm):
    norm[...] = layer_norm(latent_of(at, hidden, own, other), gain[...]).astype(bf16)
    columns = query.shape[1]
    scaled = dot(norm[...], wq[...]).astype(bf16) * (HEAD_DIM**-0.5)
    query[...] = scaled.astype(bf16)
    for weight, col in ((wk, 0), (wv, columns)):
        pair[:, col : col + columns] = dot(norm[...], weight[...]).astype(bf16)


def window_bias(queries, keys, shift):
    i = lax.broadcasted_iota(jnp.int32, (queries, keys), 0)
    j = lax.broadcasted_iota(jnp.int32, (queries, keys), 1) + shift
    return jnp.where(jnp.abs(i - j) <= WIN, 0.0, NEG).astype(f32)


def window_kernel(side, query, low, high, halo, wo, share, heads):
    band, bands = lax.axis_index("band"), lax.axis_size("band")
    rows, columns = query.shape
    end = jnp.where(band == (0 if side < 0 else bands - 1), NEG, 0.0)
    start = 0 if side < 0 else rows
    reach = -WIN if side < 0 else low.shape[0] + high.shape[0]
    places = [(low, 0), (high, low.shape[0]), (halo, reach)]
    biases = [window_bias(rows, ref.shape[0], shift - start) for ref, shift in places]
    biases[2] = biases[2] + end
    for p in range(columns // LANES):
        cols = slice(p * LANES, (p + 1) * LANES)
        vals = slice(columns + p * LANES, columns + (p + 1) * LANES)
        parts = [(ref[:, cols], ref[:, vals], b) for (ref, _), b in zip(places, biases)]
        out, total, _ = attend(query[:, cols], parts)
        heads[:, cols] = (out / total).astype(bf16)
    share[...] = dot(heads[...], wo[...]).astype(bf16)


def mixed_kernel(hidden, *refs):
    own, other, own_share, other_share = [refs[2 * i : 2 * i + 2] for i in range(4)]
    mixed = refs[-1]
    half = own[0].shape[0]
    for i in range(2):
        latent = latent_of(i * half, hidden, own[i], other[i])
        total = own_share[i][...].astype(f32) + other_share[i][...].astype(f32)
        mixed[i * half : (i + 1) * half, :] = (latent + total).astype(bf16)


def after(value, *others):
    return lax.optimization_barrier((value, *others))[0]


def shards(
    grid_latent,
    grid_gain,
    hidden_in,
    hid_gain,
    enc_wq,
    enc_wk,
    enc_wv,
    enc_wo,
    enc_edges,
    enc_counts,
    proc_gain,
    proc_wq,
    proc_wk,
    proc_wv,
    proc_wo,
):
    bands, peers = lax.axis_size("band"), lax.axis_size("mp")
    rows = grid_latent.shape[0]
    grid_band = rows * peers
    rim = grid_band // 8
    nodes, slots = enc_edges.shape
    columns = enc_wk.shape[1]
    up = [(i, i + 1) for i in range(bands - 1)]
    down = [(i + 1, i) for i in range(bands - 1)]
    grid_gain, hid_gain, proc_gain = [g.reshape(1, -1) for g in (grid_gain, hid_gain, proc_gain)]

    def shifted(value, by):
        return lax.ppermute(value, "mp", [((i + by) % peers, i) for i in range(peers)])

    if peers == 2:
        me = lambda: lax.axis_index("mp")
        cut = min(rows - rim, max(LANES, (rows - rim) // 3 * 2 // LANES * LANES))
        (ends,) = pick([grid_latent], [(0, lambda: me() * (rows - rim), rim)])
        edge = shifted(ends, 1)
        outward = [(2 * a, 2 * b) for a, b in down] + [(2 * a + 1, 2 * b + 1) for a, b in up]
        inward = [(2 * a, 2 * b) for a, b in up] + [(2 * a + 1, 2 * b + 1) for a, b in down]
        near_rim = lax.ppermute(ends, ("band", "mp"), outward)
        middle, final = pick(
            [grid_latent],
            [
                (0, lambda: (1 - me()) * rim, cut),
                (0, lambda: (1 - me()) * rim + cut, rows - rim - cut),
            ],
        )
        middle = shifted(middle, 1)
        final = shifted(final, 1)
        far_rim = lax.ppermute(edge, ("band", "mp"), inward)
        groups = [[grid_latent], [edge, middle], [final], [near_rim, far_rim]]
    else:
        me = lax.axis_index("mp")
        pieces = [grid_latent] + [shifted(grid_latent, d) for d in range(1, peers)]
        stack = jnp.stack(pieces)
        after_band = lax.dynamic_index_in_dim(stack, (-me) % peers, 0, False)[:rim]
        before_band = lax.dynamic_index_in_dim(stack, (peers - 1 - me) % peers, 0, False)[rows - rim :]
        lower = lax.ppermute(before_band, "band", up)
        upper = lax.ppermute(after_band, "band", down)
        groups = [[p] for p in pieces] + [[lower, upper]]
    sizes = [sum(p.shape[0] for p in g) for g in groups]

    *logs, query = call(
        functools.partial(prep_kernel, sizes, rows, rim, peers),
        [shape_of(nodes, s, dtype=f32) for s in sizes] + [shape_of(nodes, columns, dtype=bf16)],
        [enc_edges.T, enc_counts.reshape(1, -1), hidden_in, hid_gain, enc_wq],
        [
            pltpu.VMEM((nodes, hidden_in.shape[1]), bf16),
            pltpu.VMEM((nodes, slots), jnp.int32),
            pltpu.VMEM((nodes // 8, 8 * slots), jnp.int32),
        ],
        2 * nodes * enc_wq.size,
    )
    encode = functools.partial(grid_attention, gain=grid_gain, wk=enc_wk, wv=enc_wv, query=query)
    order = [0, 3, 1, 2] if peers == 2 else range(len(groups))
    state = None
    for i, k in enumerate(order):
        if i < len(groups) - 1:
            state = encode(groups[k], logs[k], before=state)
    half = nodes // 2
    share, keys, values = encode(groups[k], logs[k], before=state, wo=enc_wo)
    own = [share]
    own += call(
        rest_kernel,
        [shape_of(half, enc_wo.shape[1], dtype=bf16)],
        [logs[k], query, keys, values, *state, enc_wo],
        [pltpu.VMEM((half, columns), bf16)],
        2 * half * enc_wo.size,
    )

    def exchange(share):
        if peers == 2:
            return shifted(share, 1)
        return lax.psum(share.astype(f32), "mp") - share.astype(f32)

    other = [exchange(share) for share in own]
    queries, pairs = [], []
    for i in range(2):
        query, pair = call(
            functools.partial(node_kernel, i * half),
            [shape_of(half, columns, dtype=bf16), shape_of(half, 2 * columns, dtype=bf16)],
            [hidden_in, own[i], other[i], proc_gain, proc_wq, proc_wk, proc_wv],
            [pltpu.VMEM((half, hidden_in.shape[1]), bf16)],
            6 * half * proc_wq.size,
        )
        queries.append(query)
        pairs.append(pair)
    behind = lax.ppermute(pairs[0], "band", down)
    before = lax.ppermute(pairs[1], "band", up)
    shares = [None, None]
    for i, side, halo in ((1, 1, behind), (0, -1, before)):
        (shares[i],) = call(
            functools.partial(window_kernel, side),
            [shape_of(half, proc_wo.shape[1], dtype=bf16)],
            [queries[i], *pairs, halo, proc_wo],
            [pltpu.VMEM((half, columns), bf16)],
            2 * half * proc_wo.size,
        )
    other_shares = [None, None]
    for i in (1, 0):
        other_shares[i] = exchange(shares[i])
    return call(
        mixed_kernel,
        [shape_of(*hidden_in.shape, dtype=bf16)],
        [hidden_in, *own, *other, *shares, *other_shares],
    )[0]


def solution(mesh):
    return jax.shard_map(
        shards,
        mesh=mesh,
        in_specs=(
            P(("band", "mp"), None),
            P(),
            P("band", None),
            P(),
            P(None, "mp"),
            P(None, "mp"),
            P(None, "mp"),
            P("mp", None),
            P("band", None),
            P("band"),
            P(),
            P(None, "mp"),
            P(None, "mp"),
            P(None, "mp"),
            P("mp", None),
        ),
        out_specs=P("band", None),
        check_vma=False,
    )
```

```python
import functools

import jax
import jax.numpy as jnp
from jax import lax
from jax.experimental import pallas as pl
from jax.experimental.pallas import tpu as pltpu
from jax.sharding import PartitionSpec as P

D = 1024
HEADS = 16
WIN = 128
HEAD_DIM = D // HEADS
LANES = 128

EPSILON = 1e-05
NEG = -1e30
VMEM_LIMIT = 24 * 1024 * 1024

f32 = jnp.float32
bf16 = jnp.bfloat16


def whole(shape):
    return pl.BlockSpec(shape, lambda: (0,) * len(shape))


def call(kernel, outs, args, scratch=(), flops=0):
    moved = sum(a.size * a.dtype.itemsize for a in args)
    moved += sum(o.size * o.dtype.itemsize for o in outs)
    return pl.pallas_call(
        kernel,
        out_shape=outs,
        in_specs=[whole(a.shape) for a in args],
        out_specs=[whole(o.shape) for o in outs],
        scratch_shapes=list(scratch),
        compiler_params=pltpu.CompilerParams(vmem_limit_bytes=VMEM_LIMIT),
        cost_estimate=pl.CostEstimate(flops=flops, bytes_accessed=moved, transcendentals=0),
    )(*args)


def shape_of(*shape, dtype):
    return jax.ShapeDtypeStruct(shape, dtype)


def layer_norm(values, gain):
    values = values.astype(f32)
    center = values - jnp.mean(values, axis=-1, keepdims=True)
    spread = jnp.mean(center * center, axis=-1, keepdims=True)
    return center * lax.rsqrt(spread + EPSILON) * gain


def dot(a, b):
    return jnp.dot(a, b, preferred_element_type=f32)


def dot_nt(a, b):
    return lax.dot_general(a, b, (((1,), (1,)), ((), ())), preferred_element_type=f32)


def norm_rows(src, gain, dst, base, block=64):
    rows = src.shape[0]
    block = min(block, rows)

    def step(i, carry):
        at = pl.ds(pl.multiple_of(i * block, block), block)
        to = pl.ds(pl.multiple_of(base + i * block, block), block)
        dst[to, :] = layer_norm(src[at, :], gain[...]).astype(bf16)
        return carry

    lax.fori_loop(0, rows // block, step, 0, unroll=2 if rows // block % 2 == 0 else 1)


def even_lanes(rows):
    return lax.broadcasted_iota(jnp.int32, (rows, LANES), 1) < HEAD_DIM


def two_heads(pair):
    even = even_lanes(pair.shape[0])
    zero = jnp.zeros_like(pair)
    return jnp.concatenate([jnp.where(even, pair, zero), jnp.where(even, zero, pair)], axis=0)


def fold_heads(stacked):
    rows = stacked.shape[0] // 2
    return jnp.where(even_lanes(rows), stacked[:rows], stacked[rows:])


def attend(query, keys, values, bias):
    bias = jnp.concatenate([bias, bias], axis=0)
    pairs = [slice(p, p + LANES) for p in range(0, query.shape[1], LANES)]
    scores = [dot_nt(two_heads(query[:, cols]), keys[:, cols]) + bias for cols in pairs]
    tops = [jnp.max(s, axis=1, keepdims=True) for s in scores]
    weights = [jnp.exp(s - top).astype(bf16) for s, top in zip(scores, tops)]
    states = []
    for cols, part, top in zip(pairs, weights, tops):
        wide = jnp.concatenate([values[:, cols], jnp.ones_like(values[:, cols])], axis=1)
        out = dot(part, wide)
        top = jnp.broadcast_to(top, (top.shape[0], LANES))
        states.append((fold_heads(out[:, :LANES]), fold_heads(out[:, LANES:]), fold_heads(top)))
    return states


def merge(one, two):
    out1, sum1, top1 = one
    out2, sum2, top2 = two
    top = jnp.maximum(top1, top2)
    keep1 = jnp.exp(top1 - top)
    keep2 = jnp.exp(top2 - top)
    return out1 * keep1 + out2 * keep2, sum1 * keep1 + sum2 * keep2, top


def pick_kernel(cuts, whole_refs, outs, sems):
    copies = [
        pltpu.make_async_copy(
            whole_refs[k].at[pl.ds(pl.multiple_of(start(), 16), out.shape[0])], out, sems.at[i]
        )
        for i, ((k, start), out) in enumerate(zip(cuts, outs))
    ]
    for copy in copies:
        copy.start()
    for copy in copies:
        copy.wait()


def pick(arrays, cuts):
    def kernel(*refs):
        n = len(arrays)
        pick_kernel([(k, start) for k, start, _ in cuts], refs[:n], refs[n:-1], refs[-1])

    outs = [shape_of(count, arrays[k].shape[1], dtype=arrays[k].dtype) for k, _, count in cuts]
    moved = 2 * sum(o.size * o.dtype.itemsize for o in outs)
    return pl.pallas_call(
        kernel,
        out_shape=outs,
        in_specs=[pl.BlockSpec(memory_space=pltpu.HBM)] * len(arrays),
        out_specs=[whole(o.shape) for o in outs],
        scratch_shapes=[pltpu.SemaphoreType.DMA((len(cuts),))],
        compiler_params=pltpu.CompilerParams(vmem_limit_bytes=VMEM_LIMIT),
        cost_estimate=pl.CostEstimate(flops=0, bytes_accessed=moved, transcendentals=0),
    )(*arrays)


def place_of(edges, rows, rim, peers):
    band, me = lax.axis_index("band"), lax.axis_index("mp")
    grid_band = rows * peers
    at = edges - band * grid_band
    owner, inner = at // rows, at % rows
    ahead = lax.rem(owner - me + peers, peers)
    if peers == 2:
        turn = jnp.where(owner == 0, 0, rim)
        inner = jnp.where(ahead == 0, inner, (inner + turn) % rows)
        lower = grid_band + (1 - me) * rim
        upper = grid_band + me * rim
    else:
        lower = grid_band
        upper = grid_band + rim
    place = jnp.where(at < 0, lower + rim + at, ahead * rows + inner)
    return jnp.where(at >= grid_band, upper + at - grid_band, place)


def prep_kernel(sizes, rows, rim, peers, edges, counts, hidden, gain, wq, *refs):
    logs, (query, norm, turned, line) = refs[: len(sizes)], refs[len(sizes) :]
    slots, nodes = edges.shape
    share = 8
    width = share * slots
    blocks = sum(sizes) // LANES
    place = place_of(edges[...], rows, rim, peers)
    live = lax.broadcasted_iota(jnp.int32, (slots, nodes), 0) < counts[...]
    node = lax.broadcasted_iota(jnp.int32, (slots, nodes), 1) % share
    high = jnp.where(live, (place // LANES) * share + node, -1)
    turned[...] = (high * LANES + place % LANES).T
    line[...] = jnp.concatenate(
        [turned[pl.ds(i, nodes // share, stride=share), :] for i in range(share)], axis=1
    )
    row_hi = lax.broadcasted_iota(jnp.int32, (blocks * share, width), 0)
    row_lo = lax.broadcasted_iota(jnp.int32, (LANES, width), 0)

    def step(g, carry):
        code = line[pl.ds(g, 1), :]
        left = (row_hi == (code >> 7)).astype(f32).astype(bf16)
        right = (row_lo == (code & (LANES - 1))).astype(f32).astype(bf16)
        count = dot_nt(left, right)
        count = jnp.where(count > 0, jnp.log(jnp.maximum(count, 1.0)), NEG)
        to = pl.ds(pl.multiple_of(g * share, share), share)
        block = 0
        for log, size in zip(logs, sizes):
            for c in range(size // LANES):
                log[to, c * LANES : (c + 1) * LANES] = count[block * share : (block + 1) * share]
                block += 1
        return carry

    lax.fori_loop(0, nodes // share, step, 0, unroll=4)
    norm_rows(hidden, gain, norm, 0)
    scaled = dot(norm[...], wq[...]).astype(bf16) * (HEAD_DIM**-0.5)
    query[...] = scaled.astype(bf16)


def encode_heads(query, log, keys, values, before, at, heads):
    for p, state in enumerate(attend(query[at, :], keys, values, log[at, :])):
        cols = slice(p * LANES, (p + 1) * LANES)
        if before is not None:
            state = merge([b[at, cols] for b in before], state)
        heads[:, cols] = (state[0] / state[1]).astype(bf16)


def grid_kernel(count, first, last, *refs):
    refs = list(refs)
    rows = [refs.pop(0) for _ in range(count)]
    log, gain, wk, wv, query = [refs.pop(0) for _ in range(5)]
    before = None if first else [refs.pop(0) for _ in range(3)]
    if last:
        wo, share, keys, values, norm, heads = refs
    else:
        *after, norm, keys, values = refs
    base = 0
    for r in rows:
        norm_rows(r, gain, norm, base)
        base += r.shape[0]
    keys[...] = dot(norm[...], wk[...]).astype(bf16)
    values[...] = dot(norm[...], wv[...]).astype(bf16)
    if last:
        encode_heads(query, log, keys, values, before, slice(0, heads.shape[0]), heads)
        share[...] = dot(heads[...], wo[...]).astype(bf16)
        return
    for p, state in enumerate(attend(query, keys, values, log[...])):
        cols = slice(p * LANES, (p + 1) * LANES)
        if before is not None:
            state = merge([b[:, cols] for b in before], state)
        for ref, value in zip(after, state):
            ref[:, cols] = value


def grid_attention(rows, log, gain, wk, wv, query, before=None, wo=None):
    total = sum(r.shape[0] for r in rows)
    nodes, columns = query.shape
    args = [*rows, log, gain, wk, wv, query, *(before or []), *([] if wo is None else [wo])]
    pair = (total, columns)
    norm = pltpu.VMEM((total, wk.shape[0]), bf16)
    if wo is None:
        outs = [shape_of(nodes, columns, dtype=f32)] * 3
        scratch = [norm, pltpu.VMEM(pair, bf16), pltpu.VMEM(pair, bf16)]
    else:
        outs = [shape_of(nodes // 2, wo.shape[1], dtype=bf16)] + [shape_of(*pair, dtype=bf16)] * 2
        scratch = [norm, pltpu.VMEM((nodes // 2, columns), bf16)]
    kernel = functools.partial(grid_kernel, len(rows), before is None, wo is not None)
    flops = 4 * total * wk.size + 16 * nodes * total * columns
    return call(kernel, outs, args, scratch, flops)


def rest_kernel(log, query, keys, values, out, total, top, wo, share, heads):
    half = heads.shape[0]
    encode_heads(query, log, keys, values, (out, total, top), slice(half, 2 * half), heads)
    share[...] = dot(heads[...], wo[...]).astype(bf16)


def latent_of(at, hidden, own, other):
    total = own[...].astype(f32) + other[...].astype(f32)
    return hidden[at : at + own.shape[0], :].astype(f32) + total


def node_kernel(at, hidden, own, other, gain, wq, wk, wv, query, pair, norm):
    norm[...] = layer_norm(latent_of(at, hidden, own, other), gain[...]).astype(bf16)
    columns = query.shape[1]
    scaled = dot(norm[...], wq[...]).astype(bf16) * (HEAD_DIM**-0.5)
    query[...] = scaled.astype(bf16)
    for weight, col in ((wk, 0), (wv, columns)):
        pair[:, col : col + columns] = dot(norm[...], weight[...]).astype(bf16)


def window_bias(queries, keys, shift):
    i = lax.broadcasted_iota(jnp.int32, (queries, keys), 0)
    j = lax.broadcasted_iota(jnp.int32, (queries, keys), 1) + shift
    return jnp.where(jnp.abs(i - j) <= WIN, 0.0, NEG).astype(f32)


def window_kernel(side, query, low, high, halo, wo, share, heads):
    band, bands = lax.axis_index("band"), lax.axis_size("band")
    rows, columns = query.shape
    end = jnp.where(band == (0 if side < 0 else bands - 1), NEG, 0.0)
    start = 0 if side < 0 else rows
    reach = -WIN if side < 0 else low.shape[0] + high.shape[0]
    places = [(low, 0), (high, low.shape[0]), (halo, reach)]
    biases = [window_bias(rows, ref.shape[0], shift - start) for ref, shift in places]
    biases[2] = biases[2] + end
    keys, values = [
        jnp.concatenate([ref[:, at : at + columns] for ref, _ in places], axis=0) for at in (0, columns)
    ]
    for p, (out, total, _) in enumerate(attend(query, keys, values, jnp.concatenate(biases, axis=1))):
        heads[:, p * LANES : (p + 1) * LANES] = (out / total).astype(bf16)
    share[...] = dot(heads[...], wo[...]).astype(bf16)


def mixed_kernel(at, hidden, own, other, own_share, other_share, *refs):
    result, half, sem = refs[-3:]
    total = own_share[...].astype(f32) + other_share[...].astype(f32)
    half[...] = (latent_of(at, hidden, own, other) + total).astype(bf16)
    copy = pltpu.make_async_copy(half, result.at[pl.ds(at, own.shape[0]), :], sem)
    copy.start()
    copy.wait()


def mix_half(at, hidden, own, other, own_share, other_share, mixed):
    args = [hidden, own, other, own_share, other_share]
    specs = [whole(a.shape) for a in args]
    aliases = {}
    if not isinstance(mixed, jax.ShapeDtypeStruct):
        args.append(mixed)
        specs.append(pl.BlockSpec(memory_space=pltpu.HBM))
        aliases = {len(args) - 1: 0}
    return pl.pallas_call(
        functools.partial(mixed_kernel, at),
        out_shape=shape_of(*mixed.shape, dtype=mixed.dtype),
        in_specs=specs,
        out_specs=pl.BlockSpec(memory_space=pltpu.HBM),
        scratch_shapes=[pltpu.VMEM(own.shape, mixed.dtype), pltpu.SemaphoreType.DMA],
        input_output_aliases=aliases,
        compiler_params=pltpu.CompilerParams(vmem_limit_bytes=VMEM_LIMIT),
    )(*args)


def after(value, *others):
    return lax.optimization_barrier((value, *others))[0]


def shards(
    grid_latent,
    grid_gain,
    hidden_in,
    hid_gain,
    enc_wq,
    enc_wk,
    enc_wv,
    enc_wo,
    enc_edges,
    enc_counts,
    proc_gain,
    proc_wq,
    proc_wk,
    proc_wv,
    proc_wo,
):
    bands, peers = lax.axis_size("band"), lax.axis_size("mp")
    rows = grid_latent.shape[0]
    grid_band = rows * peers
    rim = grid_band // 8
    nodes, slots = enc_edges.shape
    columns = enc_wk.shape[1]
    up = [(i, i + 1) for i in range(bands - 1)]
    down = [(i + 1, i) for i in range(bands - 1)]
    grid_gain, hid_gain, proc_gain = [g.reshape(1, -1) for g in (grid_gain, hid_gain, proc_gain)]

    def shifted(value, by):
        return lax.ppermute(value, "mp", [((i + by) % peers, i) for i in range(peers)])

    if peers == 2:
        me = lambda: lax.axis_index("mp")
        cut = min(rows - rim, max(LANES, (rows - rim) // 3 * 2 // LANES * LANES))
        (ends,) = pick([grid_latent], [(0, lambda: me() * (rows - rim), rim)])
        edge = shifted(ends, 1)
        up, down = up + [(bands - 1, 0)], down + [(0, bands - 1)]
        outward = [(2 * a, 2 * b) for a, b in down] + [(2 * a + 1, 2 * b + 1) for a, b in up]
        inward = [(2 * a, 2 * b) for a, b in up] + [(2 * a + 1, 2 * b + 1) for a, b in down]
        near_rim = lax.ppermute(ends, ("band", "mp"), outward)
        middle, final = pick(
            [grid_latent],
            [
                (0, lambda: (1 - me()) * rim, cut),
                (0, lambda: (1 - me()) * rim + cut, rows - rim - cut),
            ],
        )
        middle = shifted(middle, 1)
        final = shifted(final, 1)
        groups = [[grid_latent], [edge, middle], [final], [near_rim, near_rim]]
    else:
        me = lax.axis_index("mp")
        pieces = [grid_latent] + [shifted(grid_latent, d) for d in range(1, peers)]
        stack = jnp.stack(pieces)
        after_band = lax.dynamic_index_in_dim(stack, (-me) % peers, 0, False)[:rim]
        before_band = lax.dynamic_index_in_dim(stack, (peers - 1 - me) % peers, 0, False)[rows - rim :]
        lower = lax.ppermute(before_band, "band", up)
        upper = lax.ppermute(after_band, "band", down)
        groups = [[p] for p in pieces] + [[lower, upper]]
    sizes = [sum(p.shape[0] for p in g) for g in groups]

    *logs, query = call(
        functools.partial(prep_kernel, sizes, rows, rim, peers),
        [shape_of(nodes, s, dtype=f32) for s in sizes] + [shape_of(nodes, columns, dtype=bf16)],
        [enc_edges.T, enc_counts.reshape(1, -1), hidden_in, hid_gain, enc_wq],
        [
            pltpu.VMEM((nodes, hidden_in.shape[1]), bf16),
            pltpu.VMEM((nodes, slots), jnp.int32),
            pltpu.VMEM((nodes // 8, 8 * slots), jnp.int32),
        ],
        2 * nodes * enc_wq.size,
    )
    if peers == 2:
        far_rim = lax.ppermute(after(edge, query), ("band", "mp"), inward)
        groups[3] = [near_rim, far_rim]
    encode = functools.partial(grid_attention, gain=grid_gain, wk=enc_wk, wv=enc_wv, query=query)
    order = [0, 3, 1, 2] if peers == 2 else range(len(groups))
    state = None
    for i, k in enumerate(order):
        if i < len(groups) - 1:
            state = encode(groups[k], logs[k], before=state)
    half = nodes // 2
    share, keys, values = encode(groups[k], logs[k], before=state, wo=enc_wo)
    own = [share]
    own += call(
        rest_kernel,
        [shape_of(half, enc_wo.shape[1], dtype=bf16)],
        [logs[k], query, keys, values, *state, enc_wo],
        [pltpu.VMEM((half, columns), bf16)],
        2 * half * enc_wo.size,
    )

    def exchange(share):
        if peers == 2:
            return shifted(share, 1)
        return lax.psum(share.astype(f32), "mp") - share.astype(f32)

    other = [exchange(share) for share in own]
    queries, pairs = [], []
    for i in range(2):
        query, pair = call(
            functools.partial(node_kernel, i * half),
            [shape_of(half, columns, dtype=bf16), shape_of(half, 2 * columns, dtype=bf16)],
            [hidden_in, own[i], other[i], proc_gain, proc_wq, proc_wk, proc_wv],
            [pltpu.VMEM((half, hidden_in.shape[1]), bf16)],
            6 * half * proc_wq.size,
        )
        queries.append(query)
        pairs.append(pair)
    behind = lax.ppermute(pairs[0], "band", down)
    before = lax.ppermute(pairs[1], "band", up)
    shares = [None, None]
    for i, side, halo in ((1, 1, behind), (0, -1, before)):
        (shares[i],) = call(
            functools.partial(window_kernel, side),
            [shape_of(half, proc_wo.shape[1], dtype=bf16)],
            [queries[i], *pairs, halo, proc_wo],
            [pltpu.VMEM((half, columns), bf16)],
            2 * half * proc_wo.size,
        )
    other_shares = [None, None]
    for i in (1, 0):
        other_shares[i] = exchange(shares[i])
    mixed = shape_of(*hidden_in.shape, dtype=bf16)
    for i in (1, 0):
        mixed = mix_half(i * half, hidden_in, own[i], other[i], shares[i], other_shares[i], mixed)
    return mixed


def solution(mesh):
    return jax.shard_map(
        shards,
        mesh=mesh,
        in_specs=(
            P(("band", "mp"), None),
            P(),
            P("band", None),
            P(),
            P(None, "mp"),
            P(None, "mp"),
            P(None, "mp"),
            P("mp", None),
            P("band", None),
            P("band"),
            P(),
            P(None, "mp"),
            P(None, "mp"),
            P(None, "mp"),
            P("mp", None),
        ),
        out_specs=P("band", None),
        check_vma=False,
    )
```

```python
import functools

import jax
import jax.numpy as jnp
from jax import lax
from jax.experimental import pallas as pl
from jax.experimental.pallas import tpu as pltpu
from jax.sharding import PartitionSpec as P

D = 1024
HEADS = 16
WIN = 128
HEAD_DIM = D // HEADS
LANES = 128

EPSILON = 1e-05
NEG = -1e30
PARTS = 2
VMEM_LIMIT = 24 * 1024 * 1024

f32 = jnp.float32
bf16 = jnp.bfloat16


def whole(shape):
    return pl.BlockSpec(shape, lambda: (0,) * len(shape))


def call(kernel, outs, args, scratch=(), flops=0):
    moved = sum(a.size * a.dtype.itemsize for a in args)
    moved += sum(o.size * o.dtype.itemsize for o in outs)
    return pl.pallas_call(
        kernel,
        out_shape=outs,
        in_specs=[whole(a.shape) for a in args],
        out_specs=[whole(o.shape) for o in outs],
        scratch_shapes=list(scratch),
        compiler_params=pltpu.CompilerParams(vmem_limit_bytes=VMEM_LIMIT),
        cost_estimate=pl.CostEstimate(flops=flops, bytes_accessed=moved, transcendentals=0),
    )(*args)


def shape_of(*shape, dtype):
    return jax.ShapeDtypeStruct(shape, dtype)


def layer_norm(values, gain):
    values = values.astype(f32)
    center = values - jnp.mean(values, axis=-1, keepdims=True)
    spread = jnp.mean(center * center, axis=-1, keepdims=True)
    return center * lax.rsqrt(spread + EPSILON) * gain


def dot(a, b):
    return jnp.dot(a, b, preferred_element_type=f32)


def dot_nt(a, b):
    return lax.dot_general(a, b, (((1,), (1,)), ((), ())), preferred_element_type=f32)


def norm_rows(src, gain, dst, base, block=64):
    rows = src.shape[0]
    block = min(block, rows)

    def step(i, carry):
        at = pl.ds(pl.multiple_of(i * block, block), block)
        to = pl.ds(pl.multiple_of(base + i * block, block), block)
        dst[to, :] = layer_norm(src[at, :], gain[...]).astype(bf16)
        return carry

    lax.fori_loop(0, rows // block, step, 0, unroll=2 if rows // block % 2 == 0 else 1)


def even_lanes(rows):
    return lax.broadcasted_iota(jnp.int32, (rows, LANES), 1) < HEAD_DIM


def two_heads(pair):
    even = even_lanes(pair.shape[0])
    zero = jnp.zeros_like(pair)
    return jnp.concatenate([jnp.where(even, pair, zero), jnp.where(even, zero, pair)], axis=0)


def fold_heads(stacked):
    rows = stacked.shape[0] // 2
    return jnp.where(even_lanes(rows), stacked[:rows], stacked[rows:])


def attend(query, keys, values, bias):
    bias = jnp.concatenate([bias, bias], axis=0)
    pairs = [slice(p, p + LANES) for p in range(0, query.shape[1], LANES)]
    scores = [dot_nt(two_heads(query[:, cols]), keys[:, cols]) + bias for cols in pairs]
    tops = [jnp.max(s, axis=1, keepdims=True) for s in scores]
    weights = [jnp.exp(s - top).astype(bf16) for s, top in zip(scores, tops)]
    states = []
    for cols, part, top in zip(pairs, weights, tops):
        wide = jnp.concatenate([values[:, cols], jnp.ones_like(values[:, cols])], axis=1)
        out = dot(part, wide)
        top = jnp.broadcast_to(top, (top.shape[0], LANES))
        states.append((fold_heads(out[:, :LANES]), fold_heads(out[:, LANES:]), fold_heads(top)))
    return states


def merge(one, two):
    out1, sum1, top1 = one
    out2, sum2, top2 = two
    top = jnp.maximum(top1, top2)
    keep1 = jnp.exp(top1 - top)
    keep2 = jnp.exp(top2 - top)
    return out1 * keep1 + out2 * keep2, sum1 * keep1 + sum2 * keep2, top


def pick_kernel(cuts, whole_refs, outs, sems):
    copies = [
        pltpu.make_async_copy(
            whole_refs[k].at[pl.ds(pl.multiple_of(start(), 16), out.shape[0])], out, sems.at[i]
        )
        for i, ((k, start), out) in enumerate(zip(cuts, outs))
    ]
    for copy in copies:
        copy.start()
    for copy in copies:
        copy.wait()


def pick(arrays, cuts):
    def kernel(*refs):
        n = len(arrays)
        pick_kernel([(k, start) for k, start, _ in cuts], refs[:n], refs[n:-1], refs[-1])

    outs = [shape_of(count, arrays[k].shape[1], dtype=arrays[k].dtype) for k, _, count in cuts]
    moved = 2 * sum(o.size * o.dtype.itemsize for o in outs)
    return pl.pallas_call(
        kernel,
        out_shape=outs,
        in_specs=[pl.BlockSpec(memory_space=pltpu.HBM)] * len(arrays),
        out_specs=[whole(o.shape) for o in outs],
        scratch_shapes=[pltpu.SemaphoreType.DMA((len(cuts),))],
        compiler_params=pltpu.CompilerParams(vmem_limit_bytes=VMEM_LIMIT),
        cost_estimate=pl.CostEstimate(flops=0, bytes_accessed=moved, transcendentals=0),
    )(*arrays)


def place_of(edges, rows, rim, peers):
    band, me = lax.axis_index("band"), lax.axis_index("mp")
    grid_band = rows * peers
    at = edges - band * grid_band
    owner, inner = at // rows, at % rows
    ahead = lax.rem(owner - me + peers, peers)
    if peers == 2:
        turn = jnp.where(owner == 0, 0, rim)
        inner = jnp.where(ahead == 0, inner, (inner + turn) % rows)
        lower = grid_band + (1 - me) * rim
        upper = grid_band + me * rim
    else:
        lower = grid_band
        upper = grid_band + rim
    place = jnp.where(at < 0, lower + rim + at, ahead * rows + inner)
    return jnp.where(at >= grid_band, upper + at - grid_band, place)


def prep_kernel(sizes, rows, rim, peers, edges, counts, hidden, gain, wq, *refs):
    logs, (query, norm, turned, line) = refs[: len(sizes)], refs[len(sizes) :]
    slots, nodes = edges.shape
    share = 8
    width = share * slots
    blocks = sum(sizes) // LANES
    place = place_of(edges[...], rows, rim, peers)
    live = lax.broadcasted_iota(jnp.int32, (slots, nodes), 0) < counts[...]
    node = lax.broadcasted_iota(jnp.int32, (slots, nodes), 1) % share
    high = jnp.where(live, (place // LANES) * share + node, -1)
    turned[...] = (high * LANES + place % LANES).T
    line[...] = jnp.concatenate(
        [turned[pl.ds(i, nodes // share, stride=share), :] for i in range(share)], axis=1
    )
    row_hi = lax.broadcasted_iota(jnp.int32, (blocks * share, width), 0)
    row_lo = lax.broadcasted_iota(jnp.int32, (LANES, width), 0)

    def step(g, carry):
        code = line[pl.ds(g, 1), :]
        left = (row_hi == (code >> 7)).astype(f32).astype(bf16)
        right = (row_lo == (code & (LANES - 1))).astype(f32).astype(bf16)
        count = dot_nt(left, right)
        count = jnp.where(count > 0, jnp.log(jnp.maximum(count, 1.0)), NEG)
        to = pl.ds(pl.multiple_of(g * share, share), share)
        block = 0
        for log, size in zip(logs, sizes):
            for c in range(size // LANES):
                log[to, c * LANES : (c + 1) * LANES] = count[block * share : (block + 1) * share]
                block += 1
        return carry

    lax.fori_loop(0, nodes // share, step, 0, unroll=4)
    norm_rows(hidden, gain, norm, 0)
    scaled = dot(norm[...], wq[...]).astype(bf16) * (HEAD_DIM**-0.5)
    query[...] = scaled.astype(bf16)


def encode_heads(query, log, keys, values, before, at, heads):
    for p, state in enumerate(attend(query[at, :], keys, values, log[at, :])):
        cols = slice(p * LANES, (p + 1) * LANES)
        if before is not None:
            state = merge([b[at, cols] for b in before], state)
        heads[:, cols] = (state[0] / state[1]).astype(bf16)


def grid_kernel(count, first, last, *refs):
    refs = list(refs)
    rows = [refs.pop(0) for _ in range(count)]
    log, gain, wk, wv, query = [refs.pop(0) for _ in range(5)]
    before = None if first else [refs.pop(0) for _ in range(3)]
    if last:
        wo, share, keys, values, norm, heads = refs
    else:
        *after, norm, keys, values = refs
    base = 0
    for r in rows:
        norm_rows(r, gain, norm, base)
        base += r.shape[0]
    keys[...] = dot(norm[...], wk[...]).astype(bf16)
    values[...] = dot(norm[...], wv[...]).astype(bf16)
    if last:
        encode_heads(query, log, keys, values, before, slice(0, heads.shape[0]), heads)
        share[...] = dot(heads[...], wo[...]).astype(bf16)
        return
    for p, state in enumerate(attend(query, keys, values, log[...])):
        cols = slice(p * LANES, (p + 1) * LANES)
        if before is not None:
            state = merge([b[:, cols] for b in before], state)
        for ref, value in zip(after, state):
            ref[:, cols] = value


def grid_attention(rows, log, gain, wk, wv, query, before=None, wo=None):
    total = sum(r.shape[0] for r in rows)
    nodes, columns = query.shape
    args = [*rows, log, gain, wk, wv, query, *(before or []), *([] if wo is None else [wo])]
    pair = (total, columns)
    norm = pltpu.VMEM((total, wk.shape[0]), bf16)
    if wo is None:
        outs = [shape_of(nodes, columns, dtype=f32)] * 3
        scratch = [norm, pltpu.VMEM(pair, bf16), pltpu.VMEM(pair, bf16)]
    else:
        outs = [shape_of(nodes // 2, wo.shape[1], dtype=bf16)] + [shape_of(*pair, dtype=bf16)] * 2
        scratch = [norm, pltpu.VMEM((nodes // 2, columns), bf16)]
    kernel = functools.partial(grid_kernel, len(rows), before is None, wo is not None)
    flops = 4 * total * wk.size + 16 * nodes * total * columns
    return call(kernel, outs, args, scratch, flops)


def rest_kernel(log, query, keys, values, out, total, top, wo, share, heads):
    half = heads.shape[0]
    encode_heads(query, log, keys, values, (out, total, top), slice(half, 2 * half), heads)
    share[...] = dot(heads[...], wo[...]).astype(bf16)


def latent_of(at, hidden, own, other):
    total = own[...].astype(f32) + other[...].astype(f32)
    return hidden[at : at + own.shape[0], :].astype(f32) + total


def node_kernel(at, hidden, own, other, gain, wq, wk, wv, query, pair, norm):
    norm[...] = layer_norm(latent_of(at, hidden, own, other), gain[...]).astype(bf16)
    columns = query.shape[1]
    scaled = dot(norm[...], wq[...]).astype(bf16) * (HEAD_DIM**-0.5)
    query[...] = scaled.astype(bf16)
    for weight, col in ((wk, 0), (wv, columns)):
        pair[:, col : col + columns] = dot(norm[...], weight[...]).astype(bf16)


def window_bias(queries, keys, shift):
    i = lax.broadcasted_iota(jnp.int32, (queries, keys), 0)
    j = lax.broadcasted_iota(jnp.int32, (queries, keys), 1) + shift
    return jnp.where(jnp.abs(i - j) <= WIN, 0.0, NEG).astype(f32)


def window_kernel(side, query, low, high, halo, wo, share, heads):
    band, bands = lax.axis_index("band"), lax.axis_size("band")
    rows, columns = query.shape
    end = jnp.where(band == (0 if side < 0 else bands - 1), NEG, 0.0)
    start = 0 if side < 0 else rows
    reach = -WIN if side < 0 else low.shape[0] + high.shape[0]
    places = [(low, 0), (high, low.shape[0]), (halo, reach)]
    biases = [window_bias(rows, ref.shape[0], shift - start) for ref, shift in places]
    biases[2] = biases[2] + end
    keys, values = [
        jnp.concatenate([ref[:, at : at + columns] for ref, _ in places], axis=0) for at in (0, columns)
    ]
    for p, (out, total, _) in enumerate(attend(query, keys, values, jnp.concatenate(biases, axis=1))):
        heads[:, p * LANES : (p + 1) * LANES] = (out / total).astype(bf16)
    share[...] = dot(heads[...], wo[...]).astype(bf16)


def base_kernel(at, hidden, own, other, share, base):
    base[...] = latent_of(at, hidden, own, other) + share[...].astype(f32)


def mixed_kernel(at, base, share, *refs):
    result, half, sem = refs[-3:]
    rows = base.shape[0] // PARTS
    copies = []
    for i in range(PARTS):
        part = pl.ds(i * rows, rows)
        half[part, :] = (base[part, :] + share[part, :].astype(f32)).astype(bf16)
        copies.append(
            pltpu.make_async_copy(half.at[part], result.at[pl.ds(at + i * rows, rows), :], sem.at[i])
        )
        copies[-1].start()
    for copy in copies:
        copy.wait()


def mix_half(at, base, share, mixed):
    args = [base, share]
    specs = [whole(a.shape) for a in args]
    aliases = {}
    if not isinstance(mixed, jax.ShapeDtypeStruct):
        args.append(mixed)
        specs.append(pl.BlockSpec(memory_space=pltpu.HBM))
        aliases = {len(args) - 1: 0}
    return pl.pallas_call(
        functools.partial(mixed_kernel, at),
        out_shape=shape_of(*mixed.shape, dtype=mixed.dtype),
        in_specs=specs,
        out_specs=pl.BlockSpec(memory_space=pltpu.HBM),
        scratch_shapes=[pltpu.VMEM(base.shape, mixed.dtype), pltpu.SemaphoreType.DMA((2,))],
        input_output_aliases=aliases,
        compiler_params=pltpu.CompilerParams(vmem_limit_bytes=VMEM_LIMIT),
    )(*args)


def after(value, *others):
    return lax.optimization_barrier((value, *others))[0]


def shards(
    grid_latent,
    grid_gain,
    hidden_in,
    hid_gain,
    enc_wq,
    enc_wk,
    enc_wv,
    enc_wo,
    enc_edges,
    enc_counts,
    proc_gain,
    proc_wq,
    proc_wk,
    proc_wv,
    proc_wo,
):
    bands, peers = lax.axis_size("band"), lax.axis_size("mp")
    rows = grid_latent.shape[0]
    grid_band = rows * peers
    rim = grid_band // 8
    nodes, slots = enc_edges.shape
    columns = enc_wk.shape[1]
    up = [(i, i + 1) for i in range(bands - 1)]
    down = [(i + 1, i) for i in range(bands - 1)]
    grid_gain, hid_gain, proc_gain = [g.reshape(1, -1) for g in (grid_gain, hid_gain, proc_gain)]

    def shifted(value, by):
        return lax.ppermute(value, "mp", [((i + by) % peers, i) for i in range(peers)])

    if peers == 2:
        me = lambda: lax.axis_index("mp")
        cut = min(rows - rim, max(LANES, (rows - rim) // 3 * 2 // LANES * LANES))
        ends = lax.dynamic_slice_in_dim(grid_latent, lax.axis_index("mp") * (rows - rim), rim, 0)
        edge = shifted(ends, 1)
        up, down = up + [(bands - 1, 0)], down + [(0, bands - 1)]
        outward = [(2 * a, 2 * b) for a, b in down] + [(2 * a + 1, 2 * b + 1) for a, b in up]
        inward = [(2 * a, 2 * b) for a, b in up] + [(2 * a + 1, 2 * b + 1) for a, b in down]
        near_rim = lax.ppermute(ends, ("band", "mp"), outward)
        middle, final = pick(
            [grid_latent],
            [
                (0, lambda: (1 - me()) * rim, cut),
                (0, lambda: (1 - me()) * rim + cut, rows - rim - cut),
            ],
        )
        middle = shifted(middle, 1)
        final = shifted(final, 1)
        groups = [[grid_latent], [edge, middle], [final], [near_rim, near_rim]]
    else:
        me = lax.axis_index("mp")
        pieces = [grid_latent] + [shifted(grid_latent, d) for d in range(1, peers)]
        stack = jnp.stack(pieces)
        after_band = lax.dynamic_index_in_dim(stack, (-me) % peers, 0, False)[:rim]
        before_band = lax.dynamic_index_in_dim(stack, (peers - 1 - me) % peers, 0, False)[rows - rim :]
        lower = lax.ppermute(before_band, "band", up)
        upper = lax.ppermute(after_band, "band", down)
        groups = [[p] for p in pieces] + [[lower, upper]]
    sizes = [sum(p.shape[0] for p in g) for g in groups]

    *logs, query = call(
        functools.partial(prep_kernel, sizes, rows, rim, peers),
        [shape_of(nodes, s, dtype=f32) for s in sizes] + [shape_of(nodes, columns, dtype=bf16)],
        [enc_edges.T, enc_counts.reshape(1, -1), hidden_in, hid_gain, enc_wq],
        [
            pltpu.VMEM((nodes, hidden_in.shape[1]), bf16),
            pltpu.VMEM((nodes, slots), jnp.int32),
            pltpu.VMEM((nodes // 8, 8 * slots), jnp.int32),
        ],
        2 * nodes * enc_wq.size,
    )
    if peers == 2:
        far_rim = lax.ppermute(after(edge, query), ("band", "mp"), inward)
        groups[3] = [near_rim, far_rim]
    encode = functools.partial(grid_attention, gain=grid_gain, wk=enc_wk, wv=enc_wv, query=query)
    order = [0, 3, 1, 2] if peers == 2 else range(len(groups))
    state = None
    for i, k in enumerate(order):
        if i < len(groups) - 1:
            state = encode(groups[k], logs[k], before=state)
    half = nodes // 2
    share, keys, values = encode(groups[k], logs[k], before=state, wo=enc_wo)
    own = [share]
    own += call(
        rest_kernel,
        [shape_of(half, enc_wo.shape[1], dtype=bf16)],
        [logs[k], query, keys, values, *state, enc_wo],
        [pltpu.VMEM((half, columns), bf16)],
        2 * half * enc_wo.size,
    )

    def exchange(share):
        if peers == 2:
            return shifted(share, 1)
        return lax.psum(share.astype(f32), "mp") - share.astype(f32)

    other = [exchange(share) for share in own]
    queries, pairs = [], []
    for i in range(2):
        query, pair = call(
            functools.partial(node_kernel, i * half),
            [shape_of(half, columns, dtype=bf16), shape_of(half, 2 * columns, dtype=bf16)],
            [hidden_in, own[i], other[i], proc_gain, proc_wq, proc_wk, proc_wv],
            [pltpu.VMEM((half, hidden_in.shape[1]), bf16)],
            6 * half * proc_wq.size,
        )
        queries.append(query)
        pairs.append(pair)
    behind = lax.ppermute(pairs[0], "band", down)
    before = lax.ppermute(pairs[1], "band", up)
    shares = [None, None]
    for i, side, halo in ((1, 1, behind), (0, -1, before)):
        (shares[i],) = call(
            functools.partial(window_kernel, side),
            [shape_of(half, proc_wo.shape[1], dtype=bf16)],
            [queries[i], *pairs, halo, proc_wo],
            [pltpu.VMEM((half, columns), bf16)],
            2 * half * proc_wo.size,
        )
    other_shares = [None, None]
    for i in (1, 0):
        other_shares[i] = exchange(shares[i])
    mixed = shape_of(*hidden_in.shape, dtype=bf16)
    for i in (1, 0):
        (base,) = call(
            functools.partial(base_kernel, i * half),
            [shape_of(*shares[i].shape, dtype=f32)],
            [hidden_in, own[i], other[i], shares[i]],
        )
        mixed = mix_half(i * half, base, other_shares[i], mixed)
    return mixed


def solution(mesh):
    return jax.shard_map(
        shards,
        mesh=mesh,
        in_specs=(
            P(("band", "mp"), None),
            P(),
            P("band", None),
            P(),
            P(None, "mp"),
            P(None, "mp"),
            P(None, "mp"),
            P("mp", None),
            P("band", None),
            P("band"),
            P(),
            P(None, "mp"),
            P(None, "mp"),
            P(None, "mp"),
            P("mp", None),
        ),
        out_specs=P("band", None),
        check_vma=False,
    )
```

```python
import functools

import jax
import jax.numpy as jnp
from jax import lax
from jax.experimental import pallas as pl
from jax.experimental.pallas import tpu as pltpu
from jax.sharding import PartitionSpec as P

D = 1024
HEADS = 16
WIN = 128
HEAD_DIM = D // HEADS
LANES = 128

EPSILON = 1e-05
NEG = -1e30
PARTS = 2
VMEM_LIMIT = 24 * 1024 * 1024

f32 = jnp.float32
bf16 = jnp.bfloat16


def whole(shape):
    return pl.BlockSpec(shape, lambda: (0,) * len(shape))


def call(kernel, outs, args, scratch=(), flops=0):
    moved = sum(a.size * a.dtype.itemsize for a in args)
    moved += sum(o.size * o.dtype.itemsize for o in outs)
    return pl.pallas_call(
        kernel,
        out_shape=outs,
        in_specs=[whole(a.shape) for a in args],
        out_specs=[whole(o.shape) for o in outs],
        scratch_shapes=list(scratch),
        compiler_params=pltpu.CompilerParams(vmem_limit_bytes=VMEM_LIMIT),
        cost_estimate=pl.CostEstimate(flops=flops, bytes_accessed=moved, transcendentals=0),
    )(*args)


def shape_of(*shape, dtype):
    return jax.ShapeDtypeStruct(shape, dtype)


def layer_norm(values, gain):
    values = values.astype(f32)
    center = values - jnp.mean(values, axis=-1, keepdims=True)
    spread = jnp.mean(center * center, axis=-1, keepdims=True)
    return center * lax.rsqrt(spread + EPSILON) * gain


def dot(a, b):
    return jnp.dot(a, b, preferred_element_type=f32)


def dot_nt(a, b):
    return lax.dot_general(a, b, (((1,), (1,)), ((), ())), preferred_element_type=f32)


def norm_rows(src, gain, dst, base, block=64):
    rows = src.shape[0]
    block = min(block, rows)

    def step(i, carry):
        at = pl.ds(pl.multiple_of(i * block, block), block)
        to = pl.ds(pl.multiple_of(base + i * block, block), block)
        dst[to, :] = layer_norm(src[at, :], gain[...]).astype(bf16)
        return carry

    lax.fori_loop(0, rows // block, step, 0, unroll=2 if rows // block % 2 == 0 else 1)


def even_lanes(rows):
    return lax.broadcasted_iota(jnp.int32, (rows, LANES), 1) < HEAD_DIM


def two_heads(pair):
    even = even_lanes(pair.shape[0])
    zero = jnp.zeros_like(pair)
    return jnp.concatenate([jnp.where(even, pair, zero), jnp.where(even, zero, pair)], axis=0)


def fold_heads(stacked):
    rows = stacked.shape[0] // 2
    return jnp.where(even_lanes(rows), stacked[:rows], stacked[rows:])


def attend(query, keys, values, bias):
    bias = jnp.concatenate([bias, bias], axis=0)
    pairs = [slice(p, p + LANES) for p in range(0, query.shape[1], LANES)]
    scores = [dot_nt(two_heads(query[:, cols]), keys[:, cols]) + bias for cols in pairs]
    tops = [jnp.max(s, axis=1, keepdims=True) for s in scores]
    weights = [jnp.exp(s - top).astype(bf16) for s, top in zip(scores, tops)]
    states = []
    for cols, part, top in zip(pairs, weights, tops):
        wide = jnp.concatenate([values[:, cols], jnp.ones_like(values[:, cols])], axis=1)
        out = dot(part, wide)
        top = jnp.broadcast_to(top, (top.shape[0], LANES))
        states.append((fold_heads(out[:, :LANES]), fold_heads(out[:, LANES:]), fold_heads(top)))
    return states


def merge(one, two):
    out1, sum1, top1 = one
    out2, sum2, top2 = two
    top = jnp.maximum(top1, top2)
    keep1 = jnp.exp(top1 - top)
    keep2 = jnp.exp(top2 - top)
    return out1 * keep1 + out2 * keep2, sum1 * keep1 + sum2 * keep2, top


def pick_kernel(cuts, whole_refs, outs, sems):
    copies = [
        pltpu.make_async_copy(
            whole_refs[k].at[pl.ds(pl.multiple_of(start(), 16), out.shape[0])], out, sems.at[i]
        )
        for i, ((k, start), out) in enumerate(zip(cuts, outs))
    ]
    for copy in copies:
        copy.start()
    for copy in copies:
        copy.wait()


def pick(arrays, cuts):
    def kernel(*refs):
        n = len(arrays)
        pick_kernel([(k, start) for k, start, _ in cuts], refs[:n], refs[n:-1], refs[-1])

    outs = [shape_of(count, arrays[k].shape[1], dtype=arrays[k].dtype) for k, _, count in cuts]
    moved = 2 * sum(o.size * o.dtype.itemsize for o in outs)
    return pl.pallas_call(
        kernel,
        out_shape=outs,
        in_specs=[pl.BlockSpec(memory_space=pltpu.HBM)] * len(arrays),
        out_specs=[whole(o.shape) for o in outs],
        scratch_shapes=[pltpu.SemaphoreType.DMA((len(cuts),))],
        compiler_params=pltpu.CompilerParams(vmem_limit_bytes=VMEM_LIMIT),
        cost_estimate=pl.CostEstimate(flops=0, bytes_accessed=moved, transcendentals=0),
    )(*arrays)


def place_of(edges, rows, rim, peers):
    band, me = lax.axis_index("band"), lax.axis_index("mp")
    grid_band = rows * peers
    at = edges - band * grid_band
    owner, inner = at // rows, at % rows
    ahead = lax.rem(owner - me + peers, peers)
    if peers == 2:
        turn = jnp.where(owner == 0, 0, rim)
        inner = jnp.where(ahead == 0, inner, (inner + turn) % rows)
        lower = grid_band + (1 - me) * rim
        upper = grid_band + me * rim
    else:
        lower = grid_band
        upper = grid_band + rim
    place = jnp.where(at < 0, lower + rim + at, ahead * rows + inner)
    return jnp.where(at >= grid_band, upper + at - grid_band, place)


def prep_kernel(sizes, rows, rim, peers, edges, counts, hidden, gain, wq, *refs):
    logs, (query, norm, turned, line) = refs[: len(sizes)], refs[len(sizes) :]
    slots, nodes = edges.shape
    share = 8
    width = share * slots
    blocks = sum(sizes) // LANES
    place = place_of(edges[...], rows, rim, peers)
    live = lax.broadcasted_iota(jnp.int32, (slots, nodes), 0) < counts[...]
    node = lax.broadcasted_iota(jnp.int32, (slots, nodes), 1) % share
    high = jnp.where(live, (place // LANES) * share + node, -1)
    turned[...] = (high * LANES + place % LANES).T
    line[...] = jnp.concatenate(
        [turned[pl.ds(i, nodes // share, stride=share), :] for i in range(share)], axis=1
    )
    row_hi = lax.broadcasted_iota(jnp.int32, (blocks * share, width), 0)
    row_lo = lax.broadcasted_iota(jnp.int32, (LANES, width), 0)

    def step(g, carry):
        code = line[pl.ds(g, 1), :]
        left = (row_hi == (code >> 7)).astype(f32).astype(bf16)
        right = (row_lo == (code & (LANES - 1))).astype(f32).astype(bf16)
        count = dot_nt(left, right)
        count = jnp.where(count > 0, jnp.log(jnp.maximum(count, 1.0)), NEG)
        to = pl.ds(pl.multiple_of(g * share, share), share)
        block = 0
        for log, size in zip(logs, sizes):
            for c in range(size // LANES):
                log[to, c * LANES : (c + 1) * LANES] = count[block * share : (block + 1) * share]
                block += 1
        return carry

    lax.fori_loop(0, nodes // share, step, 0, unroll=4)
    norm_rows(hidden, gain, norm, 0)
    scaled = dot(norm[...], wq[...]).astype(bf16) * (HEAD_DIM**-0.5)
    query[...] = scaled.astype(bf16)


def encode_heads(query, log, keys, values, before, at, heads):
    for p, state in enumerate(attend(query[at, :], keys, values, log[at, :])):
        cols = slice(p * LANES, (p + 1) * LANES)
        if before is not None:
            state = merge([b[at, cols] for b in before], state)
        heads[:, cols] = (state[0] / state[1]).astype(bf16)


def grid_kernel(count, first, last, *refs):
    refs = list(refs)
    rows = [refs.pop(0) for _ in range(count)]
    log, gain, wk, wv, query = [refs.pop(0) for _ in range(5)]
    before = None if first else [refs.pop(0) for _ in range(3)]
    if last:
        wo, share, keys, values, norm, heads = refs
    else:
        *after, norm, keys, values = refs
    base = 0
    for r in rows:
        norm_rows(r, gain, norm, base)
        base += r.shape[0]
    keys[...] = dot(norm[...], wk[...]).astype(bf16)
    values[...] = dot(norm[...], wv[...]).astype(bf16)
    if last:
        encode_heads(query, log, keys, values, before, slice(0, heads.shape[0]), heads)
        share[...] = dot(heads[...], wo[...]).astype(bf16)
        return
    for p, state in enumerate(attend(query, keys, values, log[...])):
        cols = slice(p * LANES, (p + 1) * LANES)
        if before is not None:
            state = merge([b[:, cols] for b in before], state)
        for ref, value in zip(after, state):
            ref[:, cols] = value


def grid_attention(rows, log, gain, wk, wv, query, before=None, wo=None):
    total = sum(r.shape[0] for r in rows)
    nodes, columns = query.shape
    args = [*rows, log, gain, wk, wv, query, *(before or []), *([] if wo is None else [wo])]
    pair = (total, columns)
    norm = pltpu.VMEM((total, wk.shape[0]), bf16)
    if wo is None:
        outs = [shape_of(nodes, columns, dtype=f32)] * 3
        scratch = [norm, pltpu.VMEM(pair, bf16), pltpu.VMEM(pair, bf16)]
    else:
        outs = [shape_of(nodes // 2, wo.shape[1], dtype=bf16)] + [shape_of(*pair, dtype=bf16)] * 2
        scratch = [norm, pltpu.VMEM((nodes // 2, columns), bf16)]
    kernel = functools.partial(grid_kernel, len(rows), before is None, wo is not None)
    flops = 4 * total * wk.size + 16 * nodes * total * columns
    return call(kernel, outs, args, scratch, flops)


def rest_kernel(log, query, keys, values, out, total, top, wo, share, heads):
    half = heads.shape[0]
    encode_heads(query, log, keys, values, (out, total, top), slice(half, 2 * half), heads)
    share[...] = dot(heads[...], wo[...]).astype(bf16)


def latent_of(at, hidden, own, other):
    total = own[...].astype(f32) + other[...].astype(f32)
    return hidden[at : at + own.shape[0], :].astype(f32) + total


def node_kernel(at, hidden, own, other, gain, wq, wk, wv, query, pair, norm):
    norm[...] = layer_norm(latent_of(at, hidden, own, other), gain[...]).astype(bf16)
    columns = query.shape[1]
    scaled = dot(norm[...], wq[...]).astype(bf16) * (HEAD_DIM**-0.5)
    query[...] = scaled.astype(bf16)
    for weight, col in ((wk, 0), (wv, columns)):
        pair[:, col : col + columns] = dot(norm[...], weight[...]).astype(bf16)


def window_bias(queries, keys, shift):
    i = lax.broadcasted_iota(jnp.int32, (queries, keys), 0)
    j = lax.broadcasted_iota(jnp.int32, (queries, keys), 1) + shift
    return jnp.where(jnp.abs(i - j) <= WIN, 0.0, NEG).astype(f32)


def window_kernel(side, query, low, high, halo, wo, share, heads):
    band, bands = lax.axis_index("band"), lax.axis_size("band")
    rows, columns = query.shape
    end = jnp.where(band == (0 if side < 0 else bands - 1), NEG, 0.0)
    start = 0 if side < 0 else rows
    reach = -WIN if side < 0 else low.shape[0] + high.shape[0]
    places = [(low, 0), (high, low.shape[0]), (halo, reach)]
    biases = [window_bias(rows, ref.shape[0], shift - start) for ref, shift in places]
    biases[2] = biases[2] + end
    keys, values = [
        jnp.concatenate([ref[:, at : at + columns] for ref, _ in places], axis=0) for at in (0, columns)
    ]
    for p, (out, total, _) in enumerate(attend(query, keys, values, jnp.concatenate(biases, axis=1))):
        heads[:, p * LANES : (p + 1) * LANES] = (out / total).astype(bf16)
    share[...] = dot(heads[...], wo[...]).astype(bf16)


def base_kernel(at, hidden, own, other, share, base):
    base[...] = latent_of(at, hidden, own, other) + share[...].astype(f32)


def mixed_kernel(at, base, share, *refs):
    result, half, sem = refs[-3:]
    rows = base.shape[0] // PARTS
    copies = []
    for i in range(PARTS):
        part = pl.ds(i * rows, rows)
        half[part, :] = (base[part, :] + share[part, :].astype(f32)).astype(bf16)
        copies.append(
            pltpu.make_async_copy(half.at[part], result.at[pl.ds(at + i * rows, rows), :], sem.at[i])
        )
        copies[-1].start()
    for copy in copies:
        copy.wait()


def mix_half(at, base, share, mixed):
    args = [base, share]
    specs = [whole(a.shape) for a in args]
    aliases = {}
    if not isinstance(mixed, jax.ShapeDtypeStruct):
        args.append(mixed)
        specs.append(pl.BlockSpec(memory_space=pltpu.HBM))
        aliases = {len(args) - 1: 0}
    return pl.pallas_call(
        functools.partial(mixed_kernel, at),
        out_shape=shape_of(*mixed.shape, dtype=mixed.dtype),
        in_specs=specs,
        out_specs=pl.BlockSpec(memory_space=pltpu.HBM),
        scratch_shapes=[pltpu.VMEM(base.shape, mixed.dtype), pltpu.SemaphoreType.DMA((2,))],
        input_output_aliases=aliases,
        compiler_params=pltpu.CompilerParams(vmem_limit_bytes=VMEM_LIMIT),
    )(*args)


def after(value, *others):
    return lax.optimization_barrier((value, *others))[0]


def shards(
    grid_latent,
    grid_gain,
    hidden_in,
    hid_gain,
    enc_wq,
    enc_wk,
    enc_wv,
    enc_wo,
    enc_edges,
    enc_counts,
    proc_gain,
    proc_wq,
    proc_wk,
    proc_wv,
    proc_wo,
):
    bands, peers = lax.axis_size("band"), lax.axis_size("mp")
    rows = grid_latent.shape[0]
    grid_band = rows * peers
    rim = grid_band // 8
    nodes, slots = enc_edges.shape
    columns = enc_wk.shape[1]
    up = [(i, i + 1) for i in range(bands - 1)]
    down = [(i + 1, i) for i in range(bands - 1)]
    grid_gain, hid_gain, proc_gain = [g.reshape(1, -1) for g in (grid_gain, hid_gain, proc_gain)]

    def shifted(value, by):
        return lax.ppermute(value, "mp", [((i + by) % peers, i) for i in range(peers)])

    if peers == 2:
        me = lambda: lax.axis_index("mp")
        cut = min(rows - rim, max(LANES, (rows - rim) // 3 * 2 // LANES * LANES))
        ends = lax.dynamic_slice_in_dim(grid_latent, lax.axis_index("mp") * (rows - rim), rim, 0)
        edge = shifted(ends, 1)
        up, down = up + [(bands - 1, 0)], down + [(0, bands - 1)]
        outward = [(2 * a, 2 * b) for a, b in down] + [(2 * a + 1, 2 * b + 1) for a, b in up]
        inward = [(2 * a, 2 * b) for a, b in up] + [(2 * a + 1, 2 * b + 1) for a, b in down]
        near_rim = lax.ppermute(ends, ("band", "mp"), outward)
        middle, final = pick(
            [grid_latent],
            [
                (0, lambda: (1 - me()) * rim, cut),
                (0, lambda: (1 - me()) * rim + cut, rows - rim - cut),
            ],
        )
        middle = shifted(middle, 1)
        final = shifted(final, 1)
        groups = [[grid_latent], [edge, middle], [final], [near_rim, near_rim]]
    else:
        me = lax.axis_index("mp")
        pieces = [grid_latent] + [shifted(grid_latent, d) for d in range(1, peers)]
        stack = jnp.stack(pieces)
        after_band = lax.dynamic_index_in_dim(stack, (-me) % peers, 0, False)[:rim]
        before_band = lax.dynamic_index_in_dim(stack, (peers - 1 - me) % peers, 0, False)[rows - rim :]
        lower = lax.ppermute(before_band, "band", up)
        upper = lax.ppermute(after_band, "band", down)
        groups = [[p] for p in pieces] + [[lower, upper]]
    sizes = [sum(p.shape[0] for p in g) for g in groups]

    *logs, query = call(
        functools.partial(prep_kernel, sizes, rows, rim, peers),
        [shape_of(nodes, s, dtype=f32) for s in sizes] + [shape_of(nodes, columns, dtype=bf16)],
        [enc_edges.T, enc_counts.reshape(1, -1), hidden_in, hid_gain, enc_wq],
        [
            pltpu.VMEM((nodes, hidden_in.shape[1]), bf16),
            pltpu.VMEM((nodes, slots), jnp.int32),
            pltpu.VMEM((nodes // 8, 8 * slots), jnp.int32),
        ],
        2 * nodes * enc_wq.size,
    )
    if peers == 2:
        far_rim = lax.ppermute(after(edge, query), ("band", "mp"), inward)
        groups[3] = [near_rim, far_rim]
    encode = functools.partial(grid_attention, gain=grid_gain, wk=enc_wk, wv=enc_wv, query=query)
    order = [0, 3, 1, 2] if peers == 2 else range(len(groups))
    state = None
    for i, k in enumerate(order):
        if i < len(groups) - 1:
            state = encode(groups[k], logs[k], before=state)
    half = nodes // 2
    share, keys, values = encode(groups[k], logs[k], before=state, wo=enc_wo)
    own = [share]
    own += call(
        rest_kernel,
        [shape_of(half, enc_wo.shape[1], dtype=bf16)],
        [logs[k], query, keys, values, *state, enc_wo],
        [pltpu.VMEM((half, columns), bf16)],
        2 * half * enc_wo.size,
    )

    def exchange(share):
        if peers == 2:
            return shifted(share, 1)
        return lax.psum(share.astype(f32), "mp") - share.astype(f32)

    other = [exchange(share) for share in own]
    queries, pairs = [], []
    for i in range(2):
        query, pair = call(
            functools.partial(node_kernel, i * half),
            [shape_of(half, columns, dtype=bf16), shape_of(half, 2 * columns, dtype=bf16)],
            [hidden_in, own[i], other[i], proc_gain, proc_wq, proc_wk, proc_wv],
            [pltpu.VMEM((half, hidden_in.shape[1]), bf16)],
            6 * half * proc_wq.size,
        )
        queries.append(query)
        pairs.append(pair)
    reach = half - WIN
    behind = lax.ppermute(pairs[0][:WIN] if reach else pairs[0], "band", down)
    before = lax.ppermute(pairs[1][reach:] if reach else pairs[1], "band", up)
    shares = [None, None]
    for i, side, halo in ((1, 1, behind), (0, -1, before)):
        (shares[i],) = call(
            functools.partial(window_kernel, side),
            [shape_of(half, proc_wo.shape[1], dtype=bf16)],
            [queries[i], *pairs, halo, proc_wo],
            [pltpu.VMEM((half, columns), bf16)],
            2 * half * proc_wo.size,
        )
    other_shares = [None, None]
    for i in (1, 0):
        other_shares[i] = exchange(shares[i])
    mixed = shape_of(*hidden_in.shape, dtype=bf16)
    for i in (1, 0):
        (base,) = call(
            functools.partial(base_kernel, i * half),
            [shape_of(*shares[i].shape, dtype=f32)],
            [hidden_in, own[i], other[i], shares[i]],
        )
        mixed = mix_half(i * half, base, other_shares[i], mixed)
    return mixed


def solution(mesh):
    return jax.shard_map(
        shards,
        mesh=mesh,
        in_specs=(
            P(("band", "mp"), None),
            P(),
            P("band", None),
            P(),
            P(None, "mp"),
            P(None, "mp"),
            P(None, "mp"),
            P("mp", None),
            P("band", None),
            P("band"),
            P(),
            P(None, "mp"),
            P(None, "mp"),
            P(None, "mp"),
            P("mp", None),
        ),
        out_specs=P("band", None),
        check_vma=False,
    )
```

```python
import functools

import jax
import jax.numpy as jnp
from jax import lax
from jax.experimental import pallas as pl
from jax.experimental.pallas import tpu as pltpu
from jax.sharding import PartitionSpec as P

D = 1024
HEADS = 16
WIN = 128
HEAD_DIM = D // HEADS
LANES = 128

EPSILON = 1e-05
NEG = -1e30
PARTS = 2
VMEM_LIMIT = 24 * 1024 * 1024

f32 = jnp.float32
bf16 = jnp.bfloat16


def whole(shape):
    return pl.BlockSpec(shape, lambda: (0,) * len(shape))


def call(kernel, outs, args, scratch=(), flops=0):
    moved = sum(a.size * a.dtype.itemsize for a in args)
    moved += sum(o.size * o.dtype.itemsize for o in outs)
    return pl.pallas_call(
        kernel,
        out_shape=outs,
        in_specs=[whole(a.shape) for a in args],
        out_specs=[whole(o.shape) for o in outs],
        scratch_shapes=list(scratch),
        compiler_params=pltpu.CompilerParams(vmem_limit_bytes=VMEM_LIMIT),
        cost_estimate=pl.CostEstimate(flops=flops, bytes_accessed=moved, transcendentals=0),
    )(*args)


def shape_of(*shape, dtype):
    return jax.ShapeDtypeStruct(shape, dtype)


def layer_norm(values, gain):
    values = values.astype(f32)
    center = values - jnp.mean(values, axis=-1, keepdims=True)
    spread = jnp.mean(center * center, axis=-1, keepdims=True)
    return center * lax.rsqrt(spread + EPSILON) * gain


def dot(a, b):
    return jnp.dot(a, b, preferred_element_type=f32)


def dot_nt(a, b):
    return lax.dot_general(a, b, (((1,), (1,)), ((), ())), preferred_element_type=f32)


def norm_rows(src, gain, dst, base, block=64):
    rows = src.shape[0]
    block = min(block, rows)

    def step(i, carry):
        at = pl.ds(pl.multiple_of(i * block, block), block)
        to = pl.ds(pl.multiple_of(base + i * block, block), block)
        dst[to, :] = layer_norm(src[at, :], gain[...]).astype(bf16)
        return carry

    lax.fori_loop(0, rows // block, step, 0, unroll=2 if rows // block % 2 == 0 else 1)


def even_lanes(rows):
    return lax.broadcasted_iota(jnp.int32, (rows, LANES), 1) < HEAD_DIM


def two_heads(pair):
    even = even_lanes(pair.shape[0])
    zero = jnp.zeros_like(pair)
    return jnp.concatenate([jnp.where(even, pair, zero), jnp.where(even, zero, pair)], axis=0)


def fold_heads(stacked):
    rows = stacked.shape[0] // 2
    return jnp.where(even_lanes(rows), stacked[:rows], stacked[rows:])


def attend(query, keys, values, bias):
    bias = jnp.concatenate([bias, bias], axis=0)
    pairs = [slice(p, p + LANES) for p in range(0, query.shape[1], LANES)]
    scores = [dot_nt(two_heads(query[:, cols]), keys[:, cols]) + bias for cols in pairs]
    tops = [jnp.max(s, axis=1, keepdims=True) for s in scores]
    weights = [jnp.exp(s - top).astype(bf16) for s, top in zip(scores, tops)]
    states = []
    for cols, part, top in zip(pairs, weights, tops):
        wide = jnp.concatenate([values[:, cols], jnp.ones_like(values[:, cols])], axis=1)
        out = dot(part, wide)
        top = jnp.broadcast_to(top, (top.shape[0], LANES))
        states.append((fold_heads(out[:, :LANES]), fold_heads(out[:, LANES:]), fold_heads(top)))
    return states


def merge(one, two):
    out1, sum1, top1 = one
    out2, sum2, top2 = two
    top = jnp.maximum(top1, top2)
    keep1 = jnp.exp(top1 - top)
    keep2 = jnp.exp(top2 - top)
    return out1 * keep1 + out2 * keep2, sum1 * keep1 + sum2 * keep2, top


def pick_kernel(cuts, whole_refs, outs, sems):
    copies = [
        pltpu.make_async_copy(
            whole_refs[k].at[pl.ds(pl.multiple_of(start(), 16), out.shape[0])], out, sems.at[i]
        )
        for i, ((k, start), out) in enumerate(zip(cuts, outs))
    ]
    for copy in copies:
        copy.start()
    for copy in copies:
        copy.wait()


def pick(arrays, cuts):
    def kernel(*refs):
        n = len(arrays)
        pick_kernel([(k, start) for k, start, _ in cuts], refs[:n], refs[n:-1], refs[-1])

    outs = [shape_of(count, arrays[k].shape[1], dtype=arrays[k].dtype) for k, _, count in cuts]
    moved = 2 * sum(o.size * o.dtype.itemsize for o in outs)
    return pl.pallas_call(
        kernel,
        out_shape=outs,
        in_specs=[pl.BlockSpec(memory_space=pltpu.HBM)] * len(arrays),
        out_specs=[whole(o.shape) for o in outs],
        scratch_shapes=[pltpu.SemaphoreType.DMA((len(cuts),))],
        compiler_params=pltpu.CompilerParams(vmem_limit_bytes=VMEM_LIMIT),
        cost_estimate=pl.CostEstimate(flops=0, bytes_accessed=moved, transcendentals=0),
    )(*arrays)


def place_of(edges, rows, rim, peers):
    band, me = lax.axis_index("band"), lax.axis_index("mp")
    grid_band = rows * peers
    at = edges - band * grid_band
    owner, inner = at // rows, at % rows
    ahead = lax.rem(owner - me + peers, peers)
    if peers == 2:
        turn = jnp.where(owner == 0, 0, rim)
        inner = jnp.where(ahead == 0, inner, (inner + turn) % rows)
        lower = grid_band + (1 - me) * rim
        upper = grid_band + me * rim
    else:
        lower = grid_band
        upper = grid_band + rim
    place = jnp.where(at < 0, lower + rim + at, ahead * rows + inner)
    return jnp.where(at >= grid_band, upper + at - grid_band, place)


def prep_kernel(sizes, rows, rim, peers, edges, counts, hidden, gain, wq, *refs):
    logs, (query, norm, turned, line) = refs[: len(sizes)], refs[len(sizes) :]
    slots, nodes = edges.shape
    share = 8
    width = share * slots
    blocks = sum(sizes) // LANES
    place = place_of(edges[...], rows, rim, peers)
    live = lax.broadcasted_iota(jnp.int32, (slots, nodes), 0) < counts[...]
    node = lax.broadcasted_iota(jnp.int32, (slots, nodes), 1) % share
    high = jnp.where(live, (place // LANES) * share + node, -1)
    turned[...] = (high * LANES + place % LANES).T
    line[...] = jnp.concatenate(
        [turned[pl.ds(i, nodes // share, stride=share), :] for i in range(share)], axis=1
    )
    row_hi = lax.broadcasted_iota(jnp.int32, (blocks * share, width), 0)
    row_lo = lax.broadcasted_iota(jnp.int32, (LANES, width), 0)

    def step(g, carry):
        code = line[pl.ds(g, 1), :]
        left = (row_hi == (code >> 7)).astype(f32).astype(bf16)
        right = (row_lo == (code & (LANES - 1))).astype(f32).astype(bf16)
        count = dot_nt(left, right)
        count = jnp.where(count > 0, jnp.log(jnp.maximum(count, 1.0)), NEG)
        to = pl.ds(pl.multiple_of(g * share, share), share)
        block = 0
        for log, size in zip(logs, sizes):
            for c in range(size // LANES):
                log[to, c * LANES : (c + 1) * LANES] = count[block * share : (block + 1) * share]
                block += 1
        return carry

    lax.fori_loop(0, nodes // share, step, 0, unroll=4)
    norm_rows(hidden, gain, norm, 0)
    scaled = dot(norm[...], wq[...]).astype(bf16) * (HEAD_DIM**-0.5)
    query[...] = scaled.astype(bf16)


def encode_heads(query, log, keys, values, before, at, heads):
    for p, state in enumerate(attend(query[at, :], keys, values, log[at, :])):
        cols = slice(p * LANES, (p + 1) * LANES)
        if before is not None:
            state = merge([b[at, cols] for b in before], state)
        heads[:, cols] = (state[0] / state[1]).astype(bf16)


def grid_kernel(count, first, last, *refs):
    refs = list(refs)
    rows = [refs.pop(0) for _ in range(count)]
    log, gain, wk, wv, query = [refs.pop(0) for _ in range(5)]
    before = None if first else [refs.pop(0) for _ in range(3)]
    if last:
        wo, share, keys, values, norm, heads = refs
    else:
        *after, norm, keys, values = refs
    base = 0
    for r in rows:
        norm_rows(r, gain, norm, base)
        base += r.shape[0]
    keys[...] = dot(norm[...], wk[...]).astype(bf16)
    values[...] = dot(norm[...], wv[...]).astype(bf16)
    if last:
        encode_heads(query, log, keys, values, before, slice(0, heads.shape[0]), heads)
        share[...] = dot(heads[...], wo[...]).astype(bf16)
        return
    for p, state in enumerate(attend(query, keys, values, log[...])):
        cols = slice(p * LANES, (p + 1) * LANES)
        if before is not None:
            state = merge([b[:, cols] for b in before], state)
        for ref, value in zip(after, state):
            ref[:, cols] = value


def grid_attention(rows, log, gain, wk, wv, query, before=None, wo=None):
    total = sum(r.shape[0] for r in rows)
    nodes, columns = query.shape
    args = [*rows, log, gain, wk, wv, query, *(before or []), *([] if wo is None else [wo])]
    pair = (total, columns)
    norm = pltpu.VMEM((total, wk.shape[0]), bf16)
    if wo is None:
        outs = [shape_of(nodes, columns, dtype=f32)] * 3
        scratch = [norm, pltpu.VMEM(pair, bf16), pltpu.VMEM(pair, bf16)]
    else:
        outs = [shape_of(nodes // 2, wo.shape[1], dtype=bf16)] + [shape_of(*pair, dtype=bf16)] * 2
        scratch = [norm, pltpu.VMEM((nodes // 2, columns), bf16)]
    kernel = functools.partial(grid_kernel, len(rows), before is None, wo is not None)
    flops = 4 * total * wk.size + 16 * nodes * total * columns
    return call(kernel, outs, args, scratch, flops)


def rest_kernel(log, query, keys, values, out, total, top, wo, share, heads):
    half = heads.shape[0]
    encode_heads(query, log, keys, values, (out, total, top), slice(half, 2 * half), heads)
    share[...] = dot(heads[...], wo[...]).astype(bf16)


def latent_of(at, hidden, own, other):
    total = own[...].astype(f32) + other[...].astype(f32)
    return hidden[at : at + own.shape[0], :].astype(f32) + total


def node_kernel(at, hidden, own, other, gain, wk, wv, norm, pair):
    norm[...] = layer_norm(latent_of(at, hidden, own, other), gain[...]).astype(bf16)
    columns = wk.shape[1]
    for weight, col in ((wk, 0), (wv, columns)):
        pair[:, col : col + columns] = dot(norm[...], weight[...]).astype(bf16)


def query_kernel(norm, wq, query):
    query[...] = (dot(norm[...], wq[...]).astype(bf16) * (HEAD_DIM**-0.5)).astype(bf16)


def window_bias(queries, keys, shift):
    i = lax.broadcasted_iota(jnp.int32, (queries, keys), 0)
    j = lax.broadcasted_iota(jnp.int32, (queries, keys), 1) + shift
    return jnp.where(jnp.abs(i - j) <= WIN, 0.0, NEG).astype(f32)


def window_kernel(side, query, low, high, halo, wo, share, heads):
    band, bands = lax.axis_index("band"), lax.axis_size("band")
    rows, columns = query.shape
    end = jnp.where(band == (0 if side < 0 else bands - 1), NEG, 0.0)
    start = 0 if side < 0 else rows
    reach = -WIN if side < 0 else low.shape[0] + high.shape[0]
    places = [(low, 0), (high, low.shape[0]), (halo, reach)]
    biases = [window_bias(rows, ref.shape[0], shift - start) for ref, shift in places]
    biases[2] = biases[2] + end
    keys, values = [
        jnp.concatenate([ref[:, at : at + columns] for ref, _ in places], axis=0) for at in (0, columns)
    ]
    for p, (out, total, _) in enumerate(attend(query, keys, values, jnp.concatenate(biases, axis=1))):
        heads[:, p * LANES : (p + 1) * LANES] = (out / total).astype(bf16)
    share[...] = dot(heads[...], wo[...]).astype(bf16)


def base_kernel(at, hidden, own, other, share, base):
    base[...] = latent_of(at, hidden, own, other) + share[...].astype(f32)


def mixed_kernel(at, base, share, *refs):
    result, half, sem = refs[-3:]
    rows = base.shape[0] // PARTS
    copies = []
    for i in range(PARTS):
        part = pl.ds(i * rows, rows)
        half[part, :] = (base[part, :] + share[part, :].astype(f32)).astype(bf16)
        copies.append(
            pltpu.make_async_copy(half.at[part], result.at[pl.ds(at + i * rows, rows), :], sem.at[i])
        )
        copies[-1].start()
    for copy in copies:
        copy.wait()


def mix_half(at, base, share, mixed):
    args = [base, share]
    specs = [whole(a.shape) for a in args]
    aliases = {}
    if not isinstance(mixed, jax.ShapeDtypeStruct):
        args.append(mixed)
        specs.append(pl.BlockSpec(memory_space=pltpu.HBM))
        aliases = {len(args) - 1: 0}
    return pl.pallas_call(
        functools.partial(mixed_kernel, at),
        out_shape=shape_of(*mixed.shape, dtype=mixed.dtype),
        in_specs=specs,
        out_specs=pl.BlockSpec(memory_space=pltpu.HBM),
        scratch_shapes=[pltpu.VMEM(base.shape, mixed.dtype), pltpu.SemaphoreType.DMA((2,))],
        input_output_aliases=aliases,
        compiler_params=pltpu.CompilerParams(vmem_limit_bytes=VMEM_LIMIT),
    )(*args)


def after(value, *others):
    return lax.optimization_barrier((value, *others))[0]


def shards(
    grid_latent,
    grid_gain,
    hidden_in,
    hid_gain,
    enc_wq,
    enc_wk,
    enc_wv,
    enc_wo,
    enc_edges,
    enc_counts,
    proc_gain,
    proc_wq,
    proc_wk,
    proc_wv,
    proc_wo,
):
    bands, peers = lax.axis_size("band"), lax.axis_size("mp")
    rows = grid_latent.shape[0]
    grid_band = rows * peers
    rim = grid_band // 8
    nodes, slots = enc_edges.shape
    columns = enc_wk.shape[1]
    up = [(i, i + 1) for i in range(bands - 1)]
    down = [(i + 1, i) for i in range(bands - 1)]
    grid_gain, hid_gain, proc_gain = [g.reshape(1, -1) for g in (grid_gain, hid_gain, proc_gain)]

    def shifted(value, by):
        return lax.ppermute(value, "mp", [((i + by) % peers, i) for i in range(peers)])

    if peers == 2:
        me = lambda: lax.axis_index("mp")
        cut = min(rows - rim, max(LANES, (rows - rim) // 3 * 2 // LANES * LANES))
        ends = lax.dynamic_slice_in_dim(grid_latent, lax.axis_index("mp") * (rows - rim), rim, 0)
        edge = shifted(ends, 1)
        up, down = up + [(bands - 1, 0)], down + [(0, bands - 1)]
        outward = [(2 * a, 2 * b) for a, b in down] + [(2 * a + 1, 2 * b + 1) for a, b in up]
        inward = [(2 * a, 2 * b) for a, b in up] + [(2 * a + 1, 2 * b + 1) for a, b in down]
        near_rim = lax.ppermute(ends, ("band", "mp"), outward)
        middle, final = pick(
            [grid_latent],
            [
                (0, lambda: (1 - me()) * rim, cut),
                (0, lambda: (1 - me()) * rim + cut, rows - rim - cut),
            ],
        )
        middle = shifted(middle, 1)
        final = shifted(final, 1)
        groups = [[grid_latent], [edge, middle], [final], [near_rim, near_rim]]
    else:
        me = lax.axis_index("mp")
        pieces = [grid_latent] + [shifted(grid_latent, d) for d in range(1, peers)]
        stack = jnp.stack(pieces)
        after_band = lax.dynamic_index_in_dim(stack, (-me) % peers, 0, False)[:rim]
        before_band = lax.dynamic_index_in_dim(stack, (peers - 1 - me) % peers, 0, False)[rows - rim :]
        lower = lax.ppermute(before_band, "band", up)
        upper = lax.ppermute(after_band, "band", down)
        groups = [[p] for p in pieces] + [[lower, upper]]
    sizes = [sum(p.shape[0] for p in g) for g in groups]

    *logs, query = call(
        functools.partial(prep_kernel, sizes, rows, rim, peers),
        [shape_of(nodes, s, dtype=f32) for s in sizes] + [shape_of(nodes, columns, dtype=bf16)],
        [enc_edges.T, enc_counts.reshape(1, -1), hidden_in, hid_gain, enc_wq],
        [
            pltpu.VMEM((nodes, hidden_in.shape[1]), bf16),
            pltpu.VMEM((nodes, slots), jnp.int32),
            pltpu.VMEM((nodes // 8, 8 * slots), jnp.int32),
        ],
        2 * nodes * enc_wq.size,
    )
    if peers == 2:
        far_rim = lax.ppermute(after(edge, query), ("band", "mp"), inward)
        groups[3] = [near_rim, far_rim]
    encode = functools.partial(grid_attention, gain=grid_gain, wk=enc_wk, wv=enc_wv, query=query)
    order = [0, 3, 1, 2] if peers == 2 else range(len(groups))
    state = None
    for i, k in enumerate(order):
        if i < len(groups) - 1:
            state = encode(groups[k], logs[k], before=state)
    half = nodes // 2
    share, keys, values = encode(groups[k], logs[k], before=state, wo=enc_wo)
    own = [share]
    own += call(
        rest_kernel,
        [shape_of(half, enc_wo.shape[1], dtype=bf16)],
        [logs[k], query, keys, values, *state, enc_wo],
        [pltpu.VMEM((half, columns), bf16)],
        2 * half * enc_wo.size,
    )

    def exchange(share):
        if peers == 2:
            return shifted(share, 1)
        return lax.psum(share.astype(f32), "mp") - share.astype(f32)

    other = [exchange(share) for share in own]
    queries, pairs = [], []
    for i in range(2):
        norm, pair = call(
            functools.partial(node_kernel, i * half),
            [shape_of(half, hidden_in.shape[1], dtype=bf16), shape_of(half, 2 * columns, dtype=bf16)],
            [hidden_in, own[i], other[i], proc_gain, proc_wk, proc_wv],
            (),
            4 * half * proc_wq.size,
        )
        (query,) = call(
            query_kernel, [shape_of(half, columns, dtype=bf16)], [norm, proc_wq], (), 2 * half * proc_wq.size
        )
        queries.append(query)
        pairs.append(pair)
    reach = half - WIN
    behind = lax.ppermute(pairs[0][:WIN] if reach else pairs[0], "band", down)
    before = lax.ppermute(pairs[1][reach:] if reach else pairs[1], "band", up)
    shares = [None, None]
    for i, side, halo in ((1, 1, behind), (0, -1, before)):
        (shares[i],) = call(
            functools.partial(window_kernel, side),
            [shape_of(half, proc_wo.shape[1], dtype=bf16)],
            [queries[i], *pairs, halo, proc_wo],
            [pltpu.VMEM((half, columns), bf16)],
            2 * half * proc_wo.size,
        )
    other_shares = [None, None]
    for i in (1, 0):
        other_shares[i] = exchange(shares[i])
    mixed = shape_of(*hidden_in.shape, dtype=bf16)
    for i in (1, 0):
        (base,) = call(
            functools.partial(base_kernel, i * half),
            [shape_of(*shares[i].shape, dtype=f32)],
            [hidden_in, own[i], other[i], shares[i]],
        )
        mixed = mix_half(i * half, base, other_shares[i], mixed)
    return mixed


def solution(mesh):
    return jax.shard_map(
        shards,
        mesh=mesh,
        in_specs=(
            P(("band", "mp"), None),
            P(),
            P("band", None),
            P(),
            P(None, "mp"),
            P(None, "mp"),
            P(None, "mp"),
            P("mp", None),
            P("band", None),
            P("band"),
            P(),
            P(None, "mp"),
            P(None, "mp"),
            P(None, "mp"),
            P("mp", None),
        ),
        out_specs=P("band", None),
        check_vma=False,
    )
```

```python
import functools

import jax
import jax.numpy as jnp
from jax import lax
from jax.experimental import pallas as pl
from jax.experimental.pallas import tpu as pltpu
from jax.sharding import PartitionSpec as P

D = 1024
HEADS = 16
WIN = 128
HEAD_DIM = D // HEADS
LANES = 128

EPSILON = 1e-05
NEG = -1e30
PARTS = 2
VMEM_LIMIT = 24 * 1024 * 1024

f32 = jnp.float32
bf16 = jnp.bfloat16


def whole(shape):
    return pl.BlockSpec(shape, lambda: (0,) * len(shape))


def call(kernel, outs, args, scratch=(), flops=0):
    moved = sum(a.size * a.dtype.itemsize for a in args)
    moved += sum(o.size * o.dtype.itemsize for o in outs)
    return pl.pallas_call(
        kernel,
        out_shape=outs,
        in_specs=[whole(a.shape) for a in args],
        out_specs=[whole(o.shape) for o in outs],
        scratch_shapes=list(scratch),
        compiler_params=pltpu.CompilerParams(vmem_limit_bytes=VMEM_LIMIT),
        cost_estimate=pl.CostEstimate(flops=flops, bytes_accessed=moved, transcendentals=0),
    )(*args)


def shape_of(*shape, dtype):
    return jax.ShapeDtypeStruct(shape, dtype)


def layer_norm(values, gain):
    values = values.astype(f32)
    center = values - jnp.mean(values, axis=-1, keepdims=True)
    spread = jnp.mean(center * center, axis=-1, keepdims=True)
    return center * lax.rsqrt(spread + EPSILON) * gain


def dot(a, b):
    return jnp.dot(a, b, preferred_element_type=f32)


def dot_nt(a, b):
    return lax.dot_general(a, b, (((1,), (1,)), ((), ())), preferred_element_type=f32)


def norm_rows(src, gain, dst, base, block=128):
    rows = src.shape[0]
    block = min(block, rows)

    def step(i, carry):
        at = pl.ds(pl.multiple_of(i * block, block), block)
        to = pl.ds(pl.multiple_of(base + i * block, block), block)
        dst[to, :] = layer_norm(src[at, :], gain[...]).astype(bf16)
        return carry

    lax.fori_loop(0, rows // block, step, 0, unroll=2 if rows // block % 2 == 0 else 1)


def even_lanes(rows):
    return lax.broadcasted_iota(jnp.int32, (rows, LANES), 1) < HEAD_DIM


def two_heads(pair):
    even = even_lanes(pair.shape[0])
    zero = jnp.zeros_like(pair)
    return jnp.concatenate([jnp.where(even, pair, zero), jnp.where(even, zero, pair)], axis=0)


def fold_heads(stacked):
    rows = stacked.shape[0] // 2
    return jnp.where(even_lanes(rows), stacked[:rows], stacked[rows:])


def attend(query, keys, values, bias):
    bias = jnp.concatenate([bias, bias], axis=0)
    pairs = [slice(p, p + LANES) for p in range(0, query.shape[1], LANES)]
    scores = [dot_nt(two_heads(query[:, cols]), keys[:, cols]) + bias for cols in pairs]
    tops = [jnp.max(s, axis=1, keepdims=True) for s in scores]
    weights = [jnp.exp(s - top).astype(bf16) for s, top in zip(scores, tops)]
    states = []
    for cols, part, top in zip(pairs, weights, tops):
        wide = jnp.concatenate([values[:, cols], jnp.ones_like(values[:, cols])], axis=1)
        out = dot(part, wide)
        top = jnp.broadcast_to(top, (top.shape[0], LANES))
        states.append((fold_heads(out[:, :LANES]), fold_heads(out[:, LANES:]), fold_heads(top)))
    return states


def merge(one, two):
    out1, sum1, top1 = one
    out2, sum2, top2 = two
    top = jnp.maximum(top1, top2)
    keep1 = jnp.exp(top1 - top)
    keep2 = jnp.exp(top2 - top)
    return out1 * keep1 + out2 * keep2, sum1 * keep1 + sum2 * keep2, top


def pick_kernel(cuts, whole_refs, outs, sems):
    copies = [
        pltpu.make_async_copy(
            whole_refs[k].at[pl.ds(pl.multiple_of(start(), 16), out.shape[0])], out, sems.at[i]
        )
        for i, ((k, start), out) in enumerate(zip(cuts, outs))
    ]
    for copy in copies:
        copy.start()
    for copy in copies:
        copy.wait()


def pick(arrays, cuts):
    def kernel(*refs):
        n = len(arrays)
        pick_kernel([(k, start) for k, start, _ in cuts], refs[:n], refs[n:-1], refs[-1])

    outs = [shape_of(count, arrays[k].shape[1], dtype=arrays[k].dtype) for k, _, count in cuts]
    moved = 2 * sum(o.size * o.dtype.itemsize for o in outs)
    return pl.pallas_call(
        kernel,
        out_shape=outs,
        in_specs=[pl.BlockSpec(memory_space=pltpu.HBM)] * len(arrays),
        out_specs=[whole(o.shape) for o in outs],
        scratch_shapes=[pltpu.SemaphoreType.DMA((len(cuts),))],
        compiler_params=pltpu.CompilerParams(vmem_limit_bytes=VMEM_LIMIT),
        cost_estimate=pl.CostEstimate(flops=0, bytes_accessed=moved, transcendentals=0),
    )(*arrays)


def place_of(edges, rows, rim, peers):
    band, me = lax.axis_index("band"), lax.axis_index("mp")
    grid_band = rows * peers
    at = edges - band * grid_band
    owner, inner = at // rows, at % rows
    ahead = lax.rem(owner - me + peers, peers)
    if peers == 2:
        turn = jnp.where(owner == 0, 0, rim)
        inner = jnp.where(ahead == 0, inner, (inner + turn) % rows)
        lower = grid_band + (1 - me) * rim
        upper = grid_band + me * rim
    else:
        lower = grid_band
        upper = grid_band + rim
    place = jnp.where(at < 0, lower + rim + at, ahead * rows + inner)
    return jnp.where(at >= grid_band, upper + at - grid_band, place)


def prep_kernel(sizes, rows, rim, peers, edges, counts, hidden, gain, wq, *refs):
    logs, (query, norm, turned, line) = refs[: len(sizes)], refs[len(sizes) :]
    slots, nodes = edges.shape
    share = 8
    width = share * slots
    blocks = sum(sizes) // LANES
    place = place_of(edges[...], rows, rim, peers)
    live = lax.broadcasted_iota(jnp.int32, (slots, nodes), 0) < counts[...]
    node = lax.broadcasted_iota(jnp.int32, (slots, nodes), 1) % share
    high = jnp.where(live, (place // LANES) * share + node, -1)
    turned[...] = (high * LANES + place % LANES).T
    line[...] = jnp.concatenate(
        [turned[pl.ds(i, nodes // share, stride=share), :] for i in range(share)], axis=1
    )
    row_hi = lax.broadcasted_iota(jnp.int32, (blocks * share, width), 0)
    row_lo = lax.broadcasted_iota(jnp.int32, (LANES, width), 0)

    def step(g, carry):
        code = line[pl.ds(g, 1), :]
        left = (row_hi == (code >> 7)).astype(f32).astype(bf16)
        right = (row_lo == (code & (LANES - 1))).astype(f32).astype(bf16)
        count = dot_nt(left, right)
        count = jnp.where(count > 0, jnp.log(jnp.maximum(count, 1.0)), NEG)
        to = pl.ds(pl.multiple_of(g * share, share), share)
        block = 0
        for log, size in zip(logs, sizes):
            for c in range(size // LANES):
                log[to, c * LANES : (c + 1) * LANES] = count[block * share : (block + 1) * share]
                block += 1
        return carry

    lax.fori_loop(0, nodes // share, step, 0, unroll=4)
    norm_rows(hidden, gain, norm, 0)
    scaled = dot(norm[...], wq[...]).astype(bf16) * (HEAD_DIM**-0.5)
    query[...] = scaled.astype(bf16)


def encode_heads(query, log, keys, values, before, at, heads):
    for p, state in enumerate(attend(query[at, :], keys, values, log[at, :])):
        cols = slice(p * LANES, (p + 1) * LANES)
        if before is not None:
            state = merge([b[at, cols] for b in before], state)
        heads[:, cols] = (state[0] / state[1]).astype(bf16)


def grid_kernel(count, first, last, *refs):
    refs = list(refs)
    rows = [refs.pop(0) for _ in range(count)]
    log, gain, wk, wv, query = [refs.pop(0) for _ in range(5)]
    before = None if first else [refs.pop(0) for _ in range(3)]
    if last:
        wo, share, keys, values, norm, heads = refs
    else:
        *after, norm, keys, values = refs
    base = 0
    for r in rows:
        norm_rows(r, gain, norm, base)
        base += r.shape[0]
    keys[...] = dot(norm[...], wk[...]).astype(bf16)
    values[...] = dot(norm[...], wv[...]).astype(bf16)
    if last:
        encode_heads(query, log, keys, values, before, slice(0, heads.shape[0]), heads)
        share[...] = dot(heads[...], wo[...]).astype(bf16)
        return
    for p, state in enumerate(attend(query, keys, values, log[...])):
        cols = slice(p * LANES, (p + 1) * LANES)
        if before is not None:
            state = merge([b[:, cols] for b in before], state)
        for ref, value in zip(after, state):
            ref[:, cols] = value


def grid_attention(rows, log, gain, wk, wv, query, before=None, wo=None):
    total = sum(r.shape[0] for r in rows)
    nodes, columns = query.shape
    args = [*rows, log, gain, wk, wv, query, *(before or []), *([] if wo is None else [wo])]
    pair = (total, columns)
    norm = pltpu.VMEM((total, wk.shape[0]), bf16)
    if wo is None:
        outs = [shape_of(nodes, columns, dtype=f32)] * 3
        scratch = [norm, pltpu.VMEM(pair, bf16), pltpu.VMEM(pair, bf16)]
    else:
        outs = [shape_of(nodes // 2, wo.shape[1], dtype=bf16)] + [shape_of(*pair, dtype=bf16)] * 2
        scratch = [norm, pltpu.VMEM((nodes // 2, columns), bf16)]
    kernel = functools.partial(grid_kernel, len(rows), before is None, wo is not None)
    flops = 4 * total * wk.size + 16 * nodes * total * columns
    return call(kernel, outs, args, scratch, flops)


def rest_kernel(log, query, keys, values, out, total, top, wo, share, heads):
    half = heads.shape[0]
    encode_heads(query, log, keys, values, (out, total, top), slice(half, 2 * half), heads)
    share[...] = dot(heads[...], wo[...]).astype(bf16)


def latent_of(at, hidden, own, other):
    total = own[...].astype(f32) + other[...].astype(f32)
    return hidden[at : at + own.shape[0], :].astype(f32) + total


def node_kernel(at, hidden, own, other, gain, wq, wk, wv, query, pair, norm):
    norm[...] = layer_norm(latent_of(at, hidden, own, other), gain[...]).astype(bf16)
    columns = query.shape[1]
    scaled = dot(norm[...], wq[...]).astype(bf16) * (HEAD_DIM**-0.5)
    query[...] = scaled.astype(bf16)
    for weight, col in ((wk, 0), (wv, columns)):
        pair[:, col : col + columns] = dot(norm[...], weight[...]).astype(bf16)


def window_bias(queries, keys, shift):
    i = lax.broadcasted_iota(jnp.int32, (queries, keys), 0)
    j = lax.broadcasted_iota(jnp.int32, (queries, keys), 1) + shift
    return jnp.where(jnp.abs(i - j) <= WIN, 0.0, NEG).astype(f32)


def window_kernel(side, query, low, high, halo, wo, share, heads):
    band, bands = lax.axis_index("band"), lax.axis_size("band")
    rows, columns = query.shape
    end = jnp.where(band == (0 if side < 0 else bands - 1), NEG, 0.0)
    start = 0 if side < 0 else rows
    reach = -WIN if side < 0 else low.shape[0] + high.shape[0]
    places = [(low, 0), (high, low.shape[0]), (halo, reach)]
    biases = [window_bias(rows, ref.shape[0], shift - start) for ref, shift in places]
    biases[2] = biases[2] + end
    keys, values = [
        jnp.concatenate([ref[:, at : at + columns] for ref, _ in places], axis=0) for at in (0, columns)
    ]
    for p, (out, total, _) in enumerate(attend(query, keys, values, jnp.concatenate(biases, axis=1))):
        heads[:, p * LANES : (p + 1) * LANES] = (out / total).astype(bf16)
    share[...] = dot(heads[...], wo[...]).astype(bf16)


def base_kernel(at, hidden, own, other, share, base):
    base[...] = latent_of(at, hidden, own, other) + share[...].astype(f32)


def mixed_kernel(at, base, share, *refs):
    result, half, sem = refs[-3:]
    rows = base.shape[0] // PARTS
    copies = []
    for i in range(PARTS):
        part = pl.ds(i * rows, rows)
        half[part, :] = (base[part, :] + share[part, :].astype(f32)).astype(bf16)
        copies.append(
            pltpu.make_async_copy(half.at[part], result.at[pl.ds(at + i * rows, rows), :], sem.at[i])
        )
        copies[-1].start()
    for copy in copies:
        copy.wait()


def mix_half(at, base, share, mixed):
    args = [base, share]
    specs = [whole(a.shape) for a in args]
    aliases = {}
    if not isinstance(mixed, jax.ShapeDtypeStruct):
        args.append(mixed)
        specs.append(pl.BlockSpec(memory_space=pltpu.HBM))
        aliases = {len(args) - 1: 0}
    return pl.pallas_call(
        functools.partial(mixed_kernel, at),
        out_shape=shape_of(*mixed.shape, dtype=mixed.dtype),
        in_specs=specs,
        out_specs=pl.BlockSpec(memory_space=pltpu.HBM),
        scratch_shapes=[pltpu.VMEM(base.shape, mixed.dtype), pltpu.SemaphoreType.DMA((2,))],
        input_output_aliases=aliases,
        compiler_params=pltpu.CompilerParams(vmem_limit_bytes=VMEM_LIMIT),
    )(*args)


def after(value, *others):
    return lax.optimization_barrier((value, *others))[0]


def shards(
    grid_latent,
    grid_gain,
    hidden_in,
    hid_gain,
    enc_wq,
    enc_wk,
    enc_wv,
    enc_wo,
    enc_edges,
    enc_counts,
    proc_gain,
    proc_wq,
    proc_wk,
    proc_wv,
    proc_wo,
):
    bands, peers = lax.axis_size("band"), lax.axis_size("mp")
    rows = grid_latent.shape[0]
    grid_band = rows * peers
    rim = grid_band // 8
    nodes, slots = enc_edges.shape
    columns = enc_wk.shape[1]
    up = [(i, i + 1) for i in range(bands - 1)]
    down = [(i + 1, i) for i in range(bands - 1)]
    grid_gain, hid_gain, proc_gain = [g.reshape(1, -1) for g in (grid_gain, hid_gain, proc_gain)]

    def shifted(value, by):
        return lax.ppermute(value, "mp", [((i + by) % peers, i) for i in range(peers)])

    if peers == 2:
        me = lambda: lax.axis_index("mp")
        cut = min(rows - rim, max(LANES, (rows - rim) // 3 * 2 // LANES * LANES))
        ends = lax.dynamic_slice_in_dim(grid_latent, lax.axis_index("mp") * (rows - rim), rim, 0)
        edge = shifted(ends, 1)
        up, down = up + [(bands - 1, 0)], down + [(0, bands - 1)]
        outward = [(2 * a, 2 * b) for a, b in down] + [(2 * a + 1, 2 * b + 1) for a, b in up]
        inward = [(2 * a, 2 * b) for a, b in up] + [(2 * a + 1, 2 * b + 1) for a, b in down]
        near_rim = lax.ppermute(ends, ("band", "mp"), outward)
        middle, final = pick(
            [grid_latent],
            [
                (0, lambda: (1 - me()) * rim, cut),
                (0, lambda: (1 - me()) * rim + cut, rows - rim - cut),
            ],
        )
        middle = shifted(middle, 1)
        final = shifted(final, 1)
        groups = [[grid_latent], [edge, middle], [final], [near_rim, near_rim]]
    else:
        me = lax.axis_index("mp")
        pieces = [grid_latent] + [shifted(grid_latent, d) for d in range(1, peers)]
        stack = jnp.stack(pieces)
        after_band = lax.dynamic_index_in_dim(stack, (-me) % peers, 0, False)[:rim]
        before_band = lax.dynamic_index_in_dim(stack, (peers - 1 - me) % peers, 0, False)[rows - rim :]
        lower = lax.ppermute(before_band, "band", up)
        upper = lax.ppermute(after_band, "band", down)
        groups = [[p] for p in pieces] + [[lower, upper]]
    sizes = [sum(p.shape[0] for p in g) for g in groups]

    *logs, query = call(
        functools.partial(prep_kernel, sizes, rows, rim, peers),
        [shape_of(nodes, s, dtype=f32) for s in sizes] + [shape_of(nodes, columns, dtype=bf16)],
        [enc_edges.T, enc_counts.reshape(1, -1), hidden_in, hid_gain, enc_wq],
        [
            pltpu.VMEM((nodes, hidden_in.shape[1]), bf16),
            pltpu.VMEM((nodes, slots), jnp.int32),
            pltpu.VMEM((nodes // 8, 8 * slots), jnp.int32),
        ],
        2 * nodes * enc_wq.size,
    )
    if peers == 2:
        far_rim = lax.ppermute(after(edge, query), ("band", "mp"), inward)
        groups[3] = [near_rim, far_rim]
    encode = functools.partial(grid_attention, gain=grid_gain, wk=enc_wk, wv=enc_wv, query=query)
    order = [0, 3, 1, 2] if peers == 2 else range(len(groups))
    state = None
    for i, k in enumerate(order):
        if i < len(groups) - 1:
            state = encode(groups[k], logs[k], before=state)
    half = nodes // 2
    share, keys, values = encode(groups[k], logs[k], before=state, wo=enc_wo)
    own = [share]
    own += call(
        rest_kernel,
        [shape_of(half, enc_wo.shape[1], dtype=bf16)],
        [logs[k], query, keys, values, *state, enc_wo],
        [pltpu.VMEM((half, columns), bf16)],
        2 * half * enc_wo.size,
    )

    def exchange(share):
        if peers == 2:
            return shifted(share, 1)
        return lax.psum(share.astype(f32), "mp") - share.astype(f32)

    other = [exchange(share) for share in own]
    queries, pairs = [], []
    for i in range(2):
        query, pair = call(
            functools.partial(node_kernel, i * half),
            [shape_of(half, columns, dtype=bf16), shape_of(half, 2 * columns, dtype=bf16)],
            [hidden_in, own[i], other[i], proc_gain, proc_wq, proc_wk, proc_wv],
            [pltpu.VMEM((half, hidden_in.shape[1]), bf16)],
            6 * half * proc_wq.size,
        )
        queries.append(query)
        pairs.append(pair)
    reach = half - WIN
    behind = lax.ppermute(pairs[0][:WIN] if reach else pairs[0], "band", down)
    before = lax.ppermute(pairs[1][reach:] if reach else pairs[1], "band", up)
    shares = [None, None]
    for i, side, halo in ((1, 1, behind), (0, -1, before)):
        (shares[i],) = call(
            functools.partial(window_kernel, side),
            [shape_of(half, proc_wo.shape[1], dtype=bf16)],
            [queries[i], *pairs, halo, proc_wo],
            [pltpu.VMEM((half, columns), bf16)],
            2 * half * proc_wo.size,
        )
    other_shares = [None, None]
    for i in (1, 0):
        other_shares[i] = exchange(shares[i])
    mixed = shape_of(*hidden_in.shape, dtype=bf16)
    for i in (1, 0):
        (base,) = call(
            functools.partial(base_kernel, i * half),
            [shape_of(*shares[i].shape, dtype=f32)],
            [hidden_in, own[i], other[i], shares[i]],
        )
        mixed = mix_half(i * half, base, other_shares[i], mixed)
    return mixed


def solution(mesh):
    return jax.shard_map(
        shards,
        mesh=mesh,
        in_specs=(
            P(("band", "mp"), None),
            P(),
            P("band", None),
            P(),
            P(None, "mp"),
            P(None, "mp"),
            P(None, "mp"),
            P("mp", None),
            P("band", None),
            P("band"),
            P(),
            P(None, "mp"),
            P(None, "mp"),
            P(None, "mp"),
            P("mp", None),
        ),
        out_specs=P("band", None),
        check_vma=False,
    )
```
